32 devices in a mesh: span: 8 (over y, x, core), freq: 4 (over z).
Axes of the slice: x: 2, y: 2, z: 4, core: 2. Of those that a mesh axis runs over, the one named last changes fastest.
Arguments:
- visibilities: bfloat16 [4, 256, 2, 512], P('freq', 'span'), may hold values from -6 to 6
- coords: float32 [4, 256, 2, 512], P('freq', 'span'), may hold values from -12 to 12
- vis_counts: int32 [4, 256], P('freq', 'span'), may hold values from 128 to 512
- cover_tile: int32 [4, 256, 1], P('freq', 'span'), may hold values from 0 to 7; in each aligned block of 32 rows (0 to 31, 32 to 63, ..., all dimensions but the last counted through in order) at most 8 rows name the same one
- offsets: int32 [4, 256, 2], P('freq', 'span'), may hold values from 0 to 96
- channel: int32 [4, 256], P('freq', 'span'), may hold values from 0 to 15
- taper: float32 [32, 32], replicated, may hold values from 0.2 to 1
Outputs:
- uv_terms: float32 [2, 8, 2, 128, 128], P(None, 'span')
The draws below stay inside these ranges and needn't reach their ends.
Inputs may be any that keep to these rules, and one draw needn't show every extreme that they name: `cover_tile`: the subgrids of one device name each tile at most 8 times, a bound that some block reaches.
All inputs are finite; a program needn't handle non-finite values.
Results may differ from the reference program's by a relative error of at most 0.005.
Values may be sent and summed in bfloat16 or wider, within the bound.
A program may use at most 64 MiB of HBM per device.

```python
import math
import jax
import jax.numpy as jnp
import numpy as np
from jax import lax

K = 512
TILE = 128
NT = 2
SUB_DEV = 32
CH_DEV = 16
CAP = 8
SUBS = 256
N_SPAN = 8
N_FREQ = 4


def set_ends(values, own_key, low, high):
    place = [jax.random.randint(jax.random.fold_in(own_key, axis), (), 0, length) for axis, length in enumerate(values.shape)]
    main_axis = values.shape.index(max(values.shape))
    beside = place[:main_axis] + [(place[main_axis] + 1) % values.shape[main_axis]] + place[main_axis + 1:]
    return values.at[tuple(place)].set(low).at[tuple(beside)].set(high)


def block_levels(own_key, extent, pieces, smallest, high):
    loudness, own = 1.0, jax.random.fold_in(own_key, 6)
    for dim, parts in pieces:
        heights = jnp.exp(jax.random.uniform(jax.random.fold_in(own, dim), (parts,), jnp.float32, smallest / len(pieces), high / len(pieces)))
        loudness = loudness * jnp.repeat(heights, extent[dim] // parts).reshape([-1 if axis == dim else 1 for axis in range(len(extent))])
    return loudness


def assign_block(rng, own, number, rows, count, top, limit, skew):
    ranking = jax.random.permutation(rng, count)
    crowded, usual = load_shares(count, rows * top, limit, skew, True), load_shares(count, rows * top, limit, skew, False)
    places = jnp.arange(count)

    def named(tallies, turn):
        used = int((tallies > 0).sum())
        fixed = max(1, used // 4)
        passed = fixed + (places - fixed + turn * (used - fixed)) % max(1, count - fixed)
        return jnp.zeros((count,), jnp.int32).at[ranking[jnp.where(places < fixed, places, passed)]].set(jnp.asarray(tallies, jnp.int32))

    tallies = jnp.where(number % 4 == 0, named(crowded, number // 4), named(usual, number - number // 4 - 1))
    mixed = jax.random.permutation(jax.random.fold_in(own, 3), count)
    source_of, receiver = mixed[0:count // 2 * 2:2], mixed[1:count // 2 * 2:2]
    room = jnp.minimum(tallies[source_of] - 1, limit - tallies[receiver]) // 2
    room = jnp.where((source_of == ranking[0]) | (receiver == ranking[0]) | (tallies[receiver] == 0), 0, jnp.maximum(room, 0))
    passed = jax.random.randint(jax.random.fold_in(own, 4), (count // 2,), 0, 1 << 20) % (room + 1)
    tallies = tallies.at[source_of].add(-passed).at[receiver].add(passed)
    items = jnp.searchsorted(jnp.cumsum(tallies), jnp.arange(rows * top), side="right").astype(jnp.int32)
    table = items.reshape(top, rows).T
    table = table[jax.random.permutation(jax.random.fold_in(own, 1), rows)]
    turn = jax.random.randint(jax.random.fold_in(own, 2), (rows, 1), 0, top)
    return jnp.take_along_axis(table, (jnp.arange(top)[None, :] + turn) % top, axis=1)


def load_shares(amount, total, bound, slope, full):
    weights = [(1 << 20) // math.isqrt(standing ** slope) + 1 for standing in range(1, amount + 1)]
    largest = bound if full else min(bound, max(-(-total // amount), total * weights[0] // sum(weights)))
    least = 1 if total - largest >= amount - 1 else 0
    given, rest = [largest] + [least] * (amount - 1), total - largest - least * (amount - 1)
    while rest > 0:
        candidates = [i for i in range(1, amount) if given[i] < largest] or [i for i in range(1, amount) if given[i] < bound]
        whole, left = sum([weights[i] for i in candidates]), rest
        for i in candidates:
            more = min(bound - given[i], max(1, left * weights[i] // whole), rest)
            given[i] = given[i] + more
            rest = rest - more
    return np.array(given)


def scatter_about(stream_key, extent, spread, reach, shards=(), kind=jnp.bfloat16):
    level = block_levels(stream_key, extent, shards, -0.22, 0.18) if shards else 1.0
    drawn = jax.random.normal(stream_key, extent, jnp.float32) * spread * level
    return jnp.minimum(jnp.maximum(drawn, -reach), reach).astype(kind)


def setup_inputs(seed: int = 0) -> dict:
    seeds = jax.random.split(jax.random.key(seed), 8)
    visibilities = scatter_about(seeds[0], (N_FREQ, SUBS, 2, K), 1.0, 6.0, ((0, 4), (1, 8)))
    coords = jnp.clip(jax.random.uniform(seeds[1], (N_FREQ, SUBS, 2, K), jnp.float32, -12.0, 12.0) * block_levels(seeds[1], (N_FREQ, SUBS, 2, K), ((0, 4), (1, 8)), -0.4, 0.0), -12.0, 12.0)
    vis_counts = set_ends(jax.random.randint(seeds[2], (N_FREQ, SUBS), K // 4, K + 1), jax.random.fold_in(seeds[2], 1), K // 4, K).astype(jnp.int32)
    cover_tile_keys = jax.random.split(jax.random.fold_in(seeds[3], 1), N_FREQ * SUBS // SUB_DEV)
    cover_tile_turns = jax.random.permutation(jax.random.fold_in(seeds[3], 3), N_FREQ * SUBS // SUB_DEV)
    cover_tile = jax.vmap(lambda own, number: assign_block(jax.random.fold_in(seeds[3], 2), own, number, SUB_DEV, N_SPAN, 1, CAP, 2))(cover_tile_keys, cover_tile_turns).reshape((N_FREQ, SUBS, 1))
    offsets = set_ends(jax.random.randint(seeds[4], (N_FREQ, SUBS, 2), 0, TILE - 31), jax.random.fold_in(seeds[4], 1), 0, (TILE - 31) - 1).astype(jnp.int32)
    channel = set_ends(jax.random.randint(seeds[5], (N_FREQ, SUBS), 0, CH_DEV), jax.random.fold_in(seeds[5], 1), 0, CH_DEV - 1).astype(jnp.int32)
    taper = jnp.clip(jnp.exp(jax.random.uniform(seeds[6], (32, 32), jnp.float32, math.log(0.2), math.log(1.0))), 0.2, 1.0)
    return dict(visibilities=visibilities, coords=coords, vis_counts=vis_counts, cover_tile=cover_tile, offsets=offsets, channel=channel, taper=taper)


def make_subgrids(vis_b, coord_b, count_b, taper):
    kk = vis_b.shape[-1]
    pix = (jnp.arange(32, dtype=jnp.float32) - 16.0) / 32.0
    live = (jnp.arange(kk, dtype=jnp.int32)[None, :] < count_b[:, None]).astype(jnp.float32)
    scale_k = 1.0 / math.sqrt(kk)
    vis_re = vis_b[:, 0, :].astype(jnp.float32) * live * scale_k
    vis_im = vis_b[:, 1, :].astype(jnp.float32) * live * scale_k
    theta_v = -2.0 * math.pi * coord_b[:, 1, :, None] * pix
    cos_v, sin_v = (jnp.cos(theta_v), jnp.sin(theta_v))
    b_re = (vis_re[:, :, None] * cos_v - vis_im[:, :, None] * sin_v).astype(jnp.bfloat16).astype(jnp.float32)
    b_im = (vis_re[:, :, None] * sin_v + vis_im[:, :, None] * cos_v).astype(jnp.bfloat16).astype(jnp.float32)
    theta_u = -2.0 * math.pi * coord_b[:, 0, :, None] * pix
    a_re = jnp.cos(theta_u).astype(jnp.bfloat16).astype(jnp.float32)
    a_im = jnp.sin(theta_u).astype(jnp.bfloat16).astype(jnp.float32)
    hp = lax.Precision.HIGHEST
    s_re = jnp.einsum('bkp,bkq->bpq', a_re, b_re, precision=hp) - jnp.einsum('bkp,bkq->bpq', a_im, b_im, precision=hp)
    s_im = jnp.einsum('bkp,bkq->bpq', a_re, b_im, precision=hp) + jnp.einsum('bkp,bkq->bpq', a_im, b_re, precision=hp)
    x_re = taper * s_re
    x_im = taper * s_im
    centred = jnp.arange(32, dtype=jnp.float32) - 16.0
    angle = -2.0 * math.pi * centred[:, None] * centred[None, :] / 32.0
    f_re, f_im = (jnp.cos(angle), jnp.sin(angle))
    y_re = jnp.einsum('ap,bpq->baq', f_re, x_re, precision=hp) - jnp.einsum('ap,bpq->baq', f_im, x_im, precision=hp)
    y_im = jnp.einsum('ap,bpq->baq', f_re, x_im, precision=hp) + jnp.einsum('ap,bpq->baq', f_im, x_re, precision=hp)
    z_re = jnp.einsum('baq,cq->bac', y_re, f_re, precision=hp) - jnp.einsum('baq,cq->bac', y_im, f_im, precision=hp)
    z_im = jnp.einsum('baq,cq->bac', y_re, f_im, precision=hp) + jnp.einsum('baq,cq->bac', y_im, f_re, precision=hp)
    return (jnp.stack([z_re, z_im], 1) / 32.0).astype(jnp.bfloat16)

def reference(visibilities, coords, vis_counts, cover_tile, offsets, channel, taper):
    n_freq = visibilities.shape[0]
    subs = visibilities.shape[1]
    n_span = subs // SUB_DEV
    channels = CH_DEV * n_freq
    size = NT * n_span * 2 * TILE * TILE
    grid0 = jnp.zeros((size,), jnp.float32)
    tt = jnp.arange(NT, dtype=jnp.int32)[:, None, None, None, None]
    cc = jnp.arange(2, dtype=jnp.int32)[None, None, :, None, None]
    pp = jnp.arange(32, dtype=jnp.int32)[None, None, None, :, None]
    qq = jnp.arange(32, dtype=jnp.int32)[None, None, None, None, :]
    powers = jnp.arange(NT, dtype=jnp.float32)

    def one_block(grid, inputs):
        vis_b, coord_b, count_b, tile_b, off_b, chan_b, fidx = inputs
        z = make_subgrids(vis_b, coord_b, count_b, taper).astype(jnp.float32)
        cg = (fidx * CH_DEV + chan_b).astype(jnp.float32)
        xval = (2.0 * cg + 1.0 - channels) / channels
        weight = jnp.where(powers[None, :] == 0.0, 1.0, xval[:, None] ** powers[None, :])
        tile_i = tile_b[:, 0].astype(jnp.int32)[None, :, None, None, None]
        row_o = off_b[:, 0].astype(jnp.int32)[None, :, None, None, None]
        col_o = off_b[:, 1].astype(jnp.int32)[None, :, None, None, None]
        idx = (((tt * n_span + tile_i) * 2 + cc) * TILE + row_o + pp) * TILE + col_o + qq
        vals = weight.T[:, :, None, None, None] * z[None]
        return (grid.at[idx.reshape(-1)].add(vals.reshape(-1)), None)
    fidx = jnp.repeat(jnp.arange(n_freq, dtype=jnp.int32), n_span)
    blocks = (visibilities.reshape(n_freq * n_span, SUB_DEV, 2, -1), coords.reshape(n_freq * n_span, SUB_DEV, 2, -1), vis_counts.reshape(n_freq * n_span, SUB_DEV), cover_tile.reshape(n_freq * n_span, SUB_DEV, 1), offsets.reshape(n_freq * n_span, SUB_DEV, 2), channel.reshape(n_freq * n_span, SUB_DEV), fidx)
    grid, _ = lax.scan(one_block, grid0, blocks)
    scale = TILE / (32.0 * math.sqrt(n_freq * SUB_DEV))
    return grid.reshape(NT, n_span, 2, TILE, TILE) * scale
```

```python
import functools
import math

import jax
import jax.numpy as jnp
import ml_dtypes
import numpy as np
from jax import lax
from jax.experimental import pallas as pl
from jax.experimental.pallas import tpu as pltpu
from jax.sharding import PartitionSpec as P

TILE = 128
NT = 2
CH_DEV = 16
SUB = 32
MESH = pl.DeviceIdType.MESH
F32 = jnp.float32
BF16 = jnp.bfloat16


def dft_constants():
    centred = np.arange(32) - 16.0
    angle = -2.0 * np.pi * centred[:, None] * centred[None, :] / 32.0
    f_re, f_im = np.cos(angle), np.sin(angle)
    right = np.block([[f_re.T, f_im.T], [-f_im.T, f_re.T]])
    right_i = np.block([[-f_im.T, f_re.T], [-f_re.T, -f_im.T]])
    both = np.concatenate([right, right_i], 1)
    left = np.block([[f_re, -f_im], [f_im, f_re]]) / 32.0
    rows, cols = np.arange(128), np.arange(512)
    repeat = (rows[:, None] // 32 == cols[None, :] // 128) & (
        rows[:, None] % 32 == cols[None, :] % 32
    )
    return [m.astype(ml_dtypes.bfloat16) for m in (both, left, repeat)]


def iota(shape, axis):
    return lax.broadcasted_iota(jnp.int32, shape, axis)


def unit_phase(turns):
    frac = turns - jnp.round(turns)
    half = frac * math.pi
    sq = half * half
    sin_h = sum_poly(sq, [(-1.0) ** n / math.factorial(2 * n + 1) for n in range(7)]) * half
    cos_h = sum_poly(sq, [(-1.0) ** n / math.factorial(2 * n) for n in range(8)])
    return 1.0 - 2.0 * sin_h * sin_h, 2.0 * sin_h * cos_h


def sum_poly(x, coefs):
    total = jnp.full_like(x, coefs[-1])
    for coef in coefs[-2::-1]:
        total = total * x + coef
    return total


def cmul(a, b):
    return a[0] * b[0] - a[1] * b[1], a[0] * b[1] + a[1] * b[0]


def kernel(
    n_span, n_freq, cap, rows_per, meta_ref, coord_ref, vis_ref, taper_ref, right_ref, left_ref,
    repeat_ref, out_ref, ea, eb, g_scr, y_scr, z_scr, src_v, src_s, send, got, acc_scr, rs_send,
    rs_got, ag_send, ag_got, src_sem, a_send, a_recv, r_send, r_recv, g_send, g_recv,
):
    me_s, me_f = lax.axis_index("span"), lax.axis_index("freq")
    barrier = pltpu.get_barrier_semaphore()
    for o in range(1, n_span):
        pl.semaphore_signal(
            barrier, inc=1, device_id=(lax.rem(me_s + o, n_span), me_f), device_id_type=MESH
        )
    for o in range(1, n_freq):
        pl.semaphore_signal(
            barrier, inc=1, device_id=(me_s, lax.rem(me_f + o, n_freq)), device_id_type=MESH
        )

    kk = coord_ref.shape[1] // 2
    lanes = cap * 32
    data_rows = cap * 16
    slots = n_span * cap

    meta = meta_ref[...].astype(F32)
    eye = iota((SUB, SUB), 0) == iota((SUB, SUB), 1)

    def to_rows(row):
        return jnp.sum(
            jnp.where(eye, jnp.broadcast_to(row, (SUB, SUB)), 0.0), axis=1, keepdims=True
        )

    dest_l = meta[3:4, :]
    dest_s = to_rows(dest_l)
    same = jnp.broadcast_to(dest_l, (SUB, SUB)) == dest_s
    lower = iota((SUB, SUB), 1) < iota((SUB, SUB), 0)
    upper = iota((SUB, SUB), 0) < iota((SUB, SUB), 1)
    rank_s = jnp.sum(jnp.where(same & lower, 1.0, 0.0), axis=1, keepdims=True)
    rank_l = jnp.sum(jnp.where(same & upper, 1.0, 0.0), axis=0, keepdims=True)
    slot_s = (dest_s * cap + rank_s).astype(jnp.int32)
    slot_l = (dest_l * cap + rank_l).astype(jnp.int32)
    hot = jnp.broadcast_to(slot_s, (SUB, 128)) == iota((SUB, 128), 1)
    src = jnp.sum(jnp.where(hot, iota((SUB, 128), 0).astype(F32), 0.0), axis=0, keepdims=True)
    src_v[...] = jnp.broadcast_to(src, (8, 128)).astype(jnp.int32)
    src_copy = pltpu.make_async_copy(src_v, src_s, src_sem)
    src_copy.start()
    col_s = to_rows(meta[7:8, :])
    count_s = to_rows(meta[8:9, :])
    hot_t = jnp.broadcast_to(slot_l, (slots, SUB)) == iota((slots, SUB), 0)
    col_splat = jnp.dot(
        jnp.where(hot_t, 1.0, 0.0).astype(BF16),
        jnp.broadcast_to(col_s, (SUB, 128)).astype(BF16),
        preferred_element_type=F32,
    )
    hot_x = jnp.broadcast_to(slot_s, (SUB, slots * 32)) == iota((SUB, slots * 32), 1) // 32
    spread_meta = jnp.dot(
        meta.astype(BF16), jnp.where(hot_x, 1.0, 0.0).astype(BF16), preferred_element_type=F32
    )
    eight = iota((8, 128), 0)
    for d in range(n_span):
        cols = col_splat[d * cap:(d + 1) * cap]
        if cap < 8:
            cols = jnp.concatenate([cols, jnp.zeros((8 - cap, 128), F32)], 0)
        info = spread_meta[0:8, d * lanes:d * lanes + 128]
        if lanes > 128:
            info = jnp.where(eight < 4, info, spread_meta[0:8, d * lanes + 128:d * lanes + 256])
        send[d, data_rows:, :] = jnp.concatenate([cols, info], 0).astype(BF16)

    def powers(turns):
        e1 = unit_phase(turns)
        e2 = cmul(e1, e1)
        e3 = cmul(e2, e1)
        e4 = cmul(e2, e2)
        e8 = cmul(e4, e4)
        e16 = cmul(e8, e8)
        return e1, e2, e3, e4, e8, e16

    def phases(i, carry):
        rows = pl.ds(pl.multiple_of(i * 8, 8), 8)
        for n, val in enumerate(powers(coord_ref[rows, 0:kk] * (-1.0 / 32.0))):
            ea[2 * n, rows, :] = val[0]
            ea[2 * n + 1, rows, :] = val[1]
        return carry

    lax.fori_loop(0, SUB // 8, phases, 0)
    e1, e2, e3, e4, e8, e16 = powers((coord_ref[:, kk:] - col_s) * (-1.0 / 32.0))
    live = jnp.where(
        iota((SUB, kk), 1).astype(F32) < jnp.broadcast_to(count_s, (SUB, kk)),
        1.0 / math.sqrt(kk), 0.0,
    )
    vis = vis_ref[...].astype(F32)
    w0 = (vis[:, :kk] * live, vis[:, kk:] * live)
    for n, val in enumerate([w0, cmul(w0, e1), cmul(w0, e2), cmul(w0, e3), e4, e8, e16]):
        eb[2 * n] = val[0]
        eb[2 * n + 1] = val[1]

    sub8 = iota((8, kk), 0)
    bit0, bit1, bit2 = lax.rem(sub8, 2) == 1, lax.rem(sub8 // 2, 2) == 1, sub8 >= 4
    taper = taper_ref[...]
    taper = jnp.concatenate([taper, taper], 1)
    taper = jnp.concatenate([taper, taper], 0)

    def expand(rows4, e4, e8, e16):
        low = [
            jnp.where(
                bit1, jnp.where(bit0, rows4[3][c], rows4[2][c]),
                jnp.where(bit0, rows4[1][c], rows4[0][c]),
            )
            for c in range(2)
        ]
        base = cmul(low, (jnp.where(bit2, e4[0], 1.0), jnp.where(bit2, e4[1], 0.0)))
        rr, ii = base[0] * e8[0], base[1] * e8[1]
        ri, ir = base[0] * e8[1], base[1] * e8[0]
        first = (base[0] * e16[0] + base[1] * e16[1], base[1] * e16[0] - base[0] * e16[1])
        blocks = [first, (rr + ii, ir - ri), base, (rr - ii, ri + ir)]
        return jnp.concatenate(
            [b[0] for b in blocks] + [b[1] for b in blocks], 0
        ).astype(BF16)

    def one_sub(s, carry):
        def row(ref, n):
            return tuple(
                jnp.broadcast_to(ref[2 * n + c, pl.ds(s, 1), :], (8, kk)) for c in range(2)
            )

        one = (jnp.ones((8, kk), F32), jnp.zeros((8, kk), F32))
        a_cat = expand([one] + [row(ea, n) for n in range(3)], *[row(ea, n) for n in range(3, 6)])
        b_cat = expand([row(eb, n) for n in range(4)], *[row(eb, n) for n in range(4, 7)])
        grid = lax.dot_general(
            a_cat, b_cat, (((1,), (1,)), ((), ())), preferred_element_type=F32
        )
        g_scr[pl.ds(pl.multiple_of(s * 64, 64), 64), :] = (grid * taper).astype(BF16)
        return carry

    lax.fori_loop(0, SUB, one_sub, 0, unroll=4)

    y_scr[...] = jnp.dot(
        g_scr[...], right_ref[...], preferred_element_type=F32
    ).astype(BF16)
    left = left_ref[...]

    def second(s, carry):
        part = jnp.dot(
            left, y_scr[pl.ds(pl.multiple_of(s * 64, 64), 64), :], preferred_element_type=F32
        )
        z_scr[s] = part[:32] + pltpu.roll(part[32:], 64, 1)
        return carry

    lax.fori_loop(0, SUB, second, 0, unroll=8)

    src_copy.wait()
    low_half = iota((32, 128), 1) < 64
    for pair in range(slots // 2):
        left_z = z_scr[jnp.clip(src_s[0, 2 * pair], 0, SUB - 1)]
        right_z = pltpu.roll(z_scr[jnp.clip(src_s[0, 2 * pair + 1], 0, SUB - 1)], 64, 1)
        d, j = pair // (cap // 2), pair % (cap // 2)
        send[d, 32 * j:32 * j + 32, :] = jnp.where(low_half, left_z, right_z).astype(BF16)

    pl.semaphore_wait(barrier, n_span + n_freq - 2)
    moves = []
    for o in range(1, n_span):
        to = lax.rem(me_s + o, n_span)
        move = pltpu.make_async_remote_copy(
            src_ref=send.at[to], dst_ref=got.at[o - 1], send_sem=a_send.at[o - 1],
            recv_sem=a_recv.at[o - 1], device_id=(to, me_f), device_id_type=MESH,
        )
        move.start()
        moves.append(move)

    channels = CH_DEV * n_freq
    lane = iota((1, 128), 1)
    lane_a = lax.rem(lane, 32).astype(F32)
    cell_row = iota((TILE, 128), 0).astype(F32)
    cell_col = iota((32, 128), 1).astype(F32)

    def place(block):
        wide = jnp.dot(block[0:data_rows, :], repeat_ref[...], preferred_element_type=F32)
        info = block[data_rows:, :].astype(F32)
        rhs = []
        for i in range(cap):
            j, h = i // 2, i % 2
            off = cell_col - jnp.broadcast_to(info[i:i + 1, :], (32, 128))
            inside = (off >= 0.0) & (off < 32.0)
            part = wide[32 * j:32 * j + 32, 256 * h:256 * h + 256]
            rhs.append(
                jnp.concatenate(
                    [jnp.where(inside, part[:, :128], 0.0), jnp.where(inside, part[:, 128:], 0.0)],
                    1,
                )
            )
        rhs = jnp.concatenate(rhs, 0).astype(BF16)
        terms = [[], [], []]
        for j in range(lanes // 128):
            at = 8 + 4 * j
            hit = cell_row == info[at:at + 1, :] + lane_a
            valid = info[at + 1:at + 2, :]
            chan = info[at + 2:at + 3, :] + (me_f * CH_DEV).astype(F32)
            xval = valid * ((2.0 * chan + 1.0 - channels) / channels)
            high = xval.astype(BF16).astype(F32)
            for t, val in enumerate([valid, high, xval - high]):
                terms[t].append(jnp.where(hit, jnp.broadcast_to(val, (TILE, 128)), 0.0))
        used = terms[:2] if channels & (channels - 1) == 0 and channels <= 256 else terms
        lhs = jnp.concatenate([jnp.concatenate(t, 1) for t in used], 0).astype(BF16)
        res = jnp.dot(lhs, rhs, preferred_element_type=F32)
        if len(used) == 3:
            res = jnp.concatenate([res[:TILE], res[TILE:2 * TILE] + res[2 * TILE:]], 0)
        return res

    acc = place(send.at[me_s])
    for o in range(1, n_span):
        moves[o - 1].wait_recv()
        acc = acc + place(got.at[o - 1])

    if n_freq * rows_per > 4 * TILE:
        pad = n_freq * rows_per - 4 * TILE
        acc_scr[4 * TILE:, :] = jnp.zeros((pad, 128), F32)
        rs_send[4 * TILE:, :] = jnp.zeros((pad, 128), BF16)
    for t in range(NT):
        for c in range(2):
            part = acc[t * TILE:(t + 1) * TILE, c * 128:(c + 1) * 128]
            at = (2 * t + c) * TILE
            acc_scr[at:at + TILE, :] = part
            rs_send[at:at + TILE, :] = part.astype(BF16)

    sums = []
    for o in range(1, n_freq):
        to = lax.rem(me_f + o, n_freq)
        move = pltpu.make_async_remote_copy(
            src_ref=rs_send.at[pl.ds(pl.multiple_of(to * rows_per, rows_per), rows_per)],
            dst_ref=rs_got.at[o - 1], send_sem=r_send.at[o - 1], recv_sem=r_recv.at[o - 1],
            device_id=(me_s, to), device_id_type=MESH,
        )
        move.start()
        sums.append(move)
    own_rows = pl.ds(pl.multiple_of(me_f * rows_per, rows_per), rows_per)
    total = acc_scr[own_rows, :]
    for o in range(1, n_freq):
        sums[o - 1].wait_recv()
        total = total + rs_got[o - 1].astype(F32)
    scale = TILE / (32.0 * math.sqrt(n_freq * SUB))
    ag_send[...] = (total * scale).astype(BF16)
    gathers = []
    for o in range(1, n_freq):
        to = lax.rem(me_f + o, n_freq)
        move = pltpu.make_async_remote_copy(
            src_ref=ag_send, dst_ref=ag_got.at[o - 1], send_sem=g_send.at[o - 1],
            recv_sem=g_recv.at[o - 1], device_id=(me_s, to), device_id_type=MESH,
        )
        move.start()
        gathers.append(move)
    out_ref[own_rows, :] = ag_send[...].astype(F32)
    for o in range(1, n_freq):
        gathers[o - 1].wait_recv()
        frm = lax.rem(me_f - o + n_freq, n_freq)
        out_ref[pl.ds(pl.multiple_of(frm * rows_per, rows_per), rows_per), :] = ag_got[
            o - 1
        ].astype(F32)
    for move in moves + sums + gathers:
        move.wait_send()


def body(visibilities, coords, vis_counts, cover_tile, offsets, channel, taper):
    n_span = lax.axis_size("span")
    n_freq = lax.axis_size("freq")
    sub = visibilities.shape[1]
    kk = visibilities.shape[-1]
    cap = max(4, 2 * sub // n_span)
    slots = n_span * cap
    rows_per = -(-4 * TILE // n_freq // 16) * 16
    while rows_per * n_freq < 4 * TILE:
        rows_per += 16
    row, col, chan = offsets[:, :, 0], offsets[:, :, 1], channel
    one, tile = jnp.ones_like(chan), cover_tile[:, :, 0]
    none = jnp.zeros((7, sub), jnp.int32)
    meta = jnp.concatenate(
        [row, one, chan, tile, row, one, chan, col, vis_counts, none], axis=0
    )
    dma = pltpu.SemaphoreType.DMA
    block = cap * 16 + 16
    out = pl.pallas_call(
        functools.partial(kernel, n_span, n_freq, cap, rows_per),
        out_shape=jax.ShapeDtypeStruct((n_freq * rows_per, 128), F32),
        in_specs=[pl.BlockSpec(memory_space=pltpu.VMEM)] * 7,
        out_specs=pl.BlockSpec(memory_space=pltpu.VMEM),
        scratch_shapes=[
            pltpu.VMEM((12, sub, kk), F32),
            pltpu.VMEM((14, sub, kk), F32),
            pltpu.VMEM((sub * 64, 64), BF16),
            pltpu.VMEM((sub * 64, 128), BF16),
            pltpu.VMEM((sub, 32, 128), F32),
            pltpu.VMEM((8, 128), jnp.int32),
            pltpu.SMEM((8, 128), jnp.int32),
            pltpu.VMEM((n_span, block, 128), BF16),
            pltpu.VMEM((n_span - 1, block, 128), BF16),
            pltpu.VMEM((n_freq * rows_per, 128), F32),
            pltpu.VMEM((n_freq * rows_per, 128), BF16),
            pltpu.VMEM((n_freq - 1, rows_per, 128), BF16),
            pltpu.VMEM((rows_per, 128), BF16),
            pltpu.VMEM((n_freq - 1, rows_per, 128), BF16),
            dma(()),
            dma((n_span - 1,)), dma((n_span - 1,)),
            dma((n_freq - 1,)), dma((n_freq - 1,)),
            dma((n_freq - 1,)), dma((n_freq - 1,)),
        ],
        compiler_params=pltpu.CompilerParams(
            collective_id=0, has_side_effects=True, vmem_limit_bytes=32 * 1024 * 1024
        ),
    )(
        meta, coords.reshape(sub, 2 * kk), visibilities.reshape(sub, 2 * kk), taper,
        *[jnp.asarray(m) for m in dft_constants()],
    )
    return out[:4 * TILE].reshape(NT, 1, 2, TILE, TILE)


def solution(mesh):
    return jax.shard_map(
        body,
        mesh=mesh,
        in_specs=(
            P("freq", "span", None, None),
            P("freq", "span", None, None),
            P("freq", "span"),
            P("freq", "span", None),
            P("freq", "span", None),
            P("freq", "span"),
            P(),
        ),
        out_specs=P(None, "span", None, None, None),
        check_vma=False,
    )
```

```python
import functools
import math

import jax
import jax.numpy as jnp
from jax import lax
from jax.experimental import pallas as pl
from jax.experimental.pallas import tpu as pltpu
from jax.sharding import PartitionSpec as P

TILE = 128
NT = 2
CH_DEV = 16
SUB = 32
MESH = pl.DeviceIdType.MESH
F32 = jnp.float32
BF16 = jnp.bfloat16


def iota(shape, axis):
    return lax.broadcasted_iota(jnp.int32, shape, axis)


def unit_phase(turns):
    frac = turns - jnp.round(turns)
    half = frac * math.pi
    sq = half * half
    sin_h = sum_poly(sq, [(-1.0) ** n / math.factorial(2 * n + 1) for n in range(7)]) * half
    cos_h = sum_poly(sq, [(-1.0) ** n / math.factorial(2 * n) for n in range(8)])
    return 1.0 - 2.0 * sin_h * sin_h, 2.0 * sin_h * cos_h


def sum_poly(x, coefs):
    total = jnp.full_like(x, coefs[-1])
    for coef in coefs[-2::-1]:
        total = total * x + coef
    return total


def cmul(a, b):
    return a[0] * b[0] - a[1] * b[1], a[0] * b[1] + a[1] * b[0]


def kernel(
    n_span, n_freq, cap, rows_per, tile_ref, offs_ref, chan_ref, count_ref, coord_ref, vis_ref,
    taper_ref, out_ref, ea, eb, g_scr, y_scr, z_scr, rhs_scr, src_v, src_s, send, got, acc_scr,
    rs_send, rs_got, ag_send, ag_got, src_sem, a_send, a_recv, r_send, r_recv, g_send, g_recv,
):
    me_s, me_f = lax.axis_index("span"), lax.axis_index("freq")
    barrier = pltpu.get_barrier_semaphore()
    for o in range(1, n_span):
        pl.semaphore_signal(
            barrier, inc=1, device_id=(lax.rem(me_s + o, n_span), me_f), device_id_type=MESH
        )
    for o in range(1, n_freq):
        pl.semaphore_signal(
            barrier, inc=1, device_id=(me_s, lax.rem(me_f + o, n_freq)), device_id_type=MESH
        )

    kk = coord_ref.shape[2]
    lanes = cap * 32
    data_rows = cap * 16
    slots = n_span * cap

    tile_l, chan_l = tile_ref[...].astype(F32), chan_ref[...].astype(F32)
    row_l, col_l = offs_ref[0:1, :].astype(F32), offs_ref[1:2, :].astype(F32)
    count_l = count_ref[...].astype(F32)
    kind = lax.rem(iota((16, SUB), 0), 4)
    meta = jnp.where(
        kind == 0, jnp.broadcast_to(row_l, (16, SUB)),
        jnp.where(kind == 1, 1.0, jnp.broadcast_to(chan_l, (16, SUB))),
    )
    eye = iota((SUB, SUB), 0) == iota((SUB, SUB), 1)

    def to_rows(row):
        return jnp.sum(
            jnp.where(eye, jnp.broadcast_to(row, (SUB, SUB)), 0.0), axis=1, keepdims=True
        )

    dest_l = tile_l
    dest_s = to_rows(dest_l)
    same = jnp.broadcast_to(dest_l, (SUB, SUB)) == dest_s
    lower = iota((SUB, SUB), 1) < iota((SUB, SUB), 0)
    upper = iota((SUB, SUB), 0) < iota((SUB, SUB), 1)
    rank_s = jnp.sum(jnp.where(same & lower, 1.0, 0.0), axis=1, keepdims=True)
    rank_l = jnp.sum(jnp.where(same & upper, 1.0, 0.0), axis=0, keepdims=True)
    slot_s = (dest_s * cap + rank_s).astype(jnp.int32)
    slot_l = (dest_l * cap + rank_l).astype(jnp.int32)
    hot = jnp.broadcast_to(slot_s, (SUB, 128)) == iota((SUB, 128), 1)
    src = jnp.sum(jnp.where(hot, iota((SUB, 128), 0).astype(F32), 0.0), axis=0, keepdims=True)
    turn_s = to_rows(col_l)
    turn_s = turn_s - 32.0 * jnp.floor(turn_s * (1.0 / 32.0))
    turn = jnp.sum(
        jnp.where(iota((SUB, 128), 0) == iota((SUB, 128), 1), turn_s, 0.0), axis=0, keepdims=True
    )
    src_v[...] = jnp.where(
        iota((8, 128), 0) == 0, jnp.broadcast_to(src, (8, 128)), jnp.broadcast_to(turn, (8, 128))
    ).astype(jnp.int32)
    src_copy = pltpu.make_async_copy(src_v, src_s, src_sem)
    src_copy.start()
    col_s = to_rows(col_l)
    count_s = to_rows(count_l)
    hot_t = jnp.broadcast_to(slot_l, (slots, SUB)) == iota((slots, SUB), 0)
    col_splat = jnp.dot(
        jnp.where(hot_t, 1.0, 0.0).astype(BF16),
        jnp.broadcast_to(col_s, (SUB, 128)).astype(BF16),
        preferred_element_type=F32,
    )
    hot_x = jnp.broadcast_to(slot_s, (SUB, slots * 32)) == iota((SUB, slots * 32), 1) // 32
    spread_meta = jnp.dot(
        meta.astype(BF16), jnp.where(hot_x, 1.0, 0.0).astype(BF16), preferred_element_type=F32
    )
    eight = iota((8, 128), 0)
    for d in range(n_span):
        cols = col_splat[d * cap:(d + 1) * cap]
        if cap < 8:
            cols = jnp.concatenate([cols, jnp.zeros((8 - cap, 128), F32)], 0)
        info = spread_meta[0:8, d * lanes:d * lanes + 128]
        if lanes > 128:
            info = jnp.where(eight < 4, info, spread_meta[0:8, d * lanes + 128:d * lanes + 256])
        send[d, data_rows:, :] = jnp.concatenate([cols, info], 0).astype(BF16)

    def powers(turns):
        e1 = unit_phase(turns)
        e2 = cmul(e1, e1)
        e3 = cmul(e2, e1)
        e4 = cmul(e2, e2)
        e8 = cmul(e4, e4)
        e16 = cmul(e8, e8)
        return e1, e2, e3, e4, e8, e16

    def phases(i, carry):
        rows = pl.ds(pl.multiple_of(i * 8, 8), 8)
        for n, val in enumerate(powers(coord_ref[rows, 0, :] * (-1.0 / 32.0))):
            ea[2 * n, rows, :] = val[0]
            ea[2 * n + 1, rows, :] = val[1]
        return carry

    lax.fori_loop(0, SUB // 8, phases, 0)
    e1, e2, e3, e4, e8, e16 = powers(coord_ref[:, 1, :] * (-1.0 / 32.0))
    live = jnp.where(
        iota((SUB, kk), 1).astype(F32) < jnp.broadcast_to(count_s, (SUB, kk)),
        1.0 / math.sqrt(kk), 0.0,
    )
    vis = vis_ref[...].astype(F32)
    w0 = (vis[:, 0, :] * live, vis[:, 1, :] * live)
    for n, val in enumerate([w0, cmul(w0, e1), cmul(w0, e2), cmul(w0, e3), e4, e8, e16]):
        eb[2 * n] = val[0]
        eb[2 * n + 1] = val[1]

    sub8 = iota((8, kk), 0)
    bit0, bit1, bit2 = lax.rem(sub8, 2) == 1, lax.rem(sub8 // 2, 2) == 1, sub8 >= 4
    taper = taper_ref[...]
    taper = jnp.concatenate([taper, taper], 1)
    taper = jnp.concatenate([taper, taper], 0)
    taper = jnp.concatenate([taper, taper], 1)
    low_half64 = iota((64, 128), 1) < 64

    def expand(rows4, e4, e8, e16):
        low = [
            jnp.where(
                bit1, jnp.where(bit0, rows4[3][c], rows4[2][c]),
                jnp.where(bit0, rows4[1][c], rows4[0][c]),
            )
            for c in range(2)
        ]
        base = cmul(low, (jnp.where(bit2, e4[0], 1.0), jnp.where(bit2, e4[1], 0.0)))
        rr, ii = base[0] * e8[0], base[1] * e8[1]
        ri, ir = base[0] * e8[1], base[1] * e8[0]
        first = (base[0] * e16[0] + base[1] * e16[1], base[1] * e16[0] - base[0] * e16[1])
        blocks = [first, (rr + ii, ir - ri), base, (rr - ii, ri + ir)]
        return jnp.concatenate(
            [b[0] for b in blocks] + [b[1] for b in blocks], 0
        ).astype(BF16)

    def one_sub(s, carry):
        def row(ref, n):
            return tuple(
                jnp.broadcast_to(ref[2 * n + c, pl.ds(s, 1), :], (8, kk)) for c in range(2)
            )

        one = (jnp.ones((8, kk), F32), jnp.zeros((8, kk), F32))
        a_cat = expand([one] + [row(ea, n) for n in range(3)], *[row(ea, n) for n in range(3, 6)])
        b_cat = expand([row(eb, n) for n in range(4)], *[row(eb, n) for n in range(4, 7)])
        grid = lax.dot_general(
            a_cat, b_cat, (((1,), (1,)), ((), ())), preferred_element_type=F32
        )
        wide = jnp.concatenate([grid, grid], 1) * taper
        high = wide.astype(BF16)
        rest = (wide - high.astype(F32)).astype(BF16)
        rows = pl.ds(pl.multiple_of(s * 64, 64), 64)
        g_scr[rows, 0:128] = high
        g_scr[rows, 128:256] = rest
        return carry

    lax.fori_loop(0, SUB, one_sub, 0, unroll=4)

    def turns_of(rows, cols):
        prod = (lax.rem(rows, 32) - 16) * (lax.rem(cols, 32) - 16)
        return prod.astype(F32) * (-1.0 / 32.0)

    def quarter(n):
        return n.astype(F32) * 0.25

    rows, cols = iota((64, 128), 0), iota((64, 128), 1)
    right = unit_phase(
        turns_of(rows, cols) + quarter(cols // 64 + rows // 32 - lax.rem(cols // 32, 2))
    )[0]
    right_h = right.astype(BF16)
    right_l = (right - right_h.astype(F32)).astype(BF16)
    right = jnp.concatenate([right_h, right_l, right_h, jnp.zeros((64, 128), BF16)], 0)
    rows, cols = iota((64, 64), 0), iota((64, 64), 1)
    left = unit_phase(turns_of(rows, cols) + quarter(cols // 32 - rows // 32))[0]
    left = (left * (1.0 / 32.0)).astype(BF16)
    rows, cols = iota((128, 512), 0), iota((128, 512), 1)
    repeat = jnp.where(
        (rows // 32 == cols // 128) & (lax.rem(rows, 32) == lax.rem(cols, 32)), 1.0, 0.0
    ).astype(BF16)

    y_scr[...] = jnp.dot(g_scr[...], right, preferred_element_type=F32).astype(BF16)
    lane32 = lax.rem(iota((32, 128), 1), 32)
    src_copy.wait()

    def second(s, carry):
        part = jnp.dot(
            left, y_scr[pl.ds(pl.multiple_of(s * 64, 64), 64), :], preferred_element_type=F32
        )
        sub = part[:32] + pltpu.roll(part[32:], 64, 1)
        turn = jnp.clip(src_s[1, s], 0, 31)
        z_scr[s] = jnp.where(
            lane32 >= turn, pltpu.roll(sub, turn, 1), pltpu.roll(sub, turn + 96, 1)
        )
        return carry

    lax.fori_loop(0, SUB, second, 0, unroll=8)

    low_half = iota((32, 128), 1) < 64
    for pair in range(slots // 2):
        left_z = z_scr[jnp.clip(src_s[0, 2 * pair], 0, SUB - 1)]
        right_z = pltpu.roll(z_scr[jnp.clip(src_s[0, 2 * pair + 1], 0, SUB - 1)], 64, 1)
        d, j = pair // (cap // 2), pair % (cap // 2)
        send[d, 32 * j:32 * j + 32, :] = jnp.where(low_half, left_z, right_z).astype(BF16)

    pl.semaphore_wait(barrier, n_span + n_freq - 2)
    moves = []
    for o in range(1, n_span):
        to = lax.rem(me_s + o, n_span)
        move = pltpu.make_async_remote_copy(
            src_ref=send.at[to], dst_ref=got.at[o - 1], send_sem=a_send.at[o - 1],
            recv_sem=a_recv.at[o - 1], device_id=(to, me_f), device_id_type=MESH,
        )
        move.start()
        moves.append(move)

    channels = CH_DEV * n_freq
    lane = iota((1, 128), 1)
    lane_a = lax.rem(lane, 32).astype(F32)
    cell_row = iota((TILE, 128), 0).astype(F32)
    cell_col = iota((32, 128), 1).astype(F32)

    def widen(block, n):
        wide = jnp.dot(block[0:data_rows, :], repeat, preferred_element_type=F32)
        info = block[data_rows:, :].astype(F32)
        for i in range(cap):
            j, h = i // 2, i % 2
            off = cell_col - jnp.broadcast_to(info[i:i + 1, :], (32, 128))
            inside = (off >= 0.0) & (off < 32.0)
            part = wide[32 * j:32 * j + 32, 256 * h:256 * h + 256]
            rhs_scr[n, 32 * i:32 * i + 32, 0:128] = jnp.where(
                inside, part[:, :128], 0.0
            ).astype(BF16)
            rhs_scr[n, 32 * i:32 * i + 32, 128:256] = jnp.where(
                inside, part[:, 128:], 0.0
            ).astype(BF16)

    exact = channels & (channels - 1) == 0 and channels <= 256

    def weigh(block, n, term):
        info = block[data_rows:, :].astype(F32)
        high, low = [], []
        for j in range(lanes // 128):
            at = 8 + 4 * j
            hit = cell_row == info[at:at + 1, :] + lane_a
            val = info[at + 1:at + 2, :]
            if term == 1:
                chan = info[at + 2:at + 3, :] + (me_f * CH_DEV).astype(F32)
                val = val * ((2.0 * chan + 1.0 - channels) / channels)
            cut = val.astype(BF16).astype(F32)
            high.append(jnp.where(hit, jnp.broadcast_to(cut, (TILE, 128)), 0.0).astype(BF16))
            low.append(jnp.where(hit, jnp.broadcast_to(val - cut, (TILE, 128)), 0.0).astype(BF16))
        res = jnp.dot(jnp.concatenate(high, 1), rhs_scr[n], preferred_element_type=F32)
        if term == 1 and not exact:
            res = res + jnp.dot(jnp.concatenate(low, 1), rhs_scr[n], preferred_element_type=F32)
        return res

    blocks = [send.at[me_s]] + [got.at[o - 1] for o in range(1, n_span)]
    acc = None
    for n, block in enumerate(blocks):
        if n:
            moves[n - 1].wait_recv()
        widen(block, n)
        res = weigh(block, n, 0)
        acc = res if acc is None else acc + res

    def peer_rows(place):
        return pl.ds(pl.multiple_of(place * rows_per, rows_per), rows_per)

    half = 2 * TILE
    pad = n_freq * rows_per - half

    def scatter(acc, term):
        if pad:
            acc_scr[term, half:, :] = jnp.zeros((pad, 128), F32)
            rs_send[term, half:, :] = jnp.zeros((pad, 128), BF16)
        for c in range(2):
            part = acc[:, c * 128:(c + 1) * 128]
            acc_scr[term, c * TILE:(c + 1) * TILE, :] = part
            rs_send[term, c * TILE:(c + 1) * TILE, :] = part.astype(BF16)
        started = []
        for o in range(1, n_freq):
            to = lax.rem(me_f + o, n_freq)
            move = pltpu.make_async_remote_copy(
                src_ref=rs_send.at[term, peer_rows(to)], dst_ref=rs_got.at[term, o - 1],
                send_sem=r_send.at[term, o - 1], recv_sem=r_recv.at[term, o - 1],
                device_id=(me_s, to), device_id_type=MESH,
            )
            move.start()
            started.append(move)
        return started

    sums = [scatter(acc, 0)]
    acc = None
    for n, block in enumerate(blocks):
        res = weigh(block, n, 1)
        acc = res if acc is None else acc + res
    sums.append(scatter(acc, 1))

    scale = TILE / (32.0 * math.sqrt(n_freq * SUB))
    gathers = []
    for term in range(NT):
        total = acc_scr[term, peer_rows(me_f), :]
        for o in range(1, n_freq):
            sums[term][o - 1].wait_recv()
            total = total + rs_got[term, o - 1].astype(F32)
        ag_send[term] = (total * scale).astype(BF16)
        started = []
        for o in range(1, n_freq):
            to = lax.rem(me_f + o, n_freq)
            move = pltpu.make_async_remote_copy(
                src_ref=ag_send.at[term], dst_ref=ag_got.at[term, o - 1],
                send_sem=g_send.at[term, o - 1], recv_sem=g_recv.at[term, o - 1],
                device_id=(me_s, to), device_id_type=MESH,
            )
            move.start()
            started.append(move)
        gathers.append(started)
        out_ref[term, peer_rows(me_f), :] = ag_send[term].astype(F32)
    for term in range(NT):
        for o in range(1, n_freq):
            gathers[term][o - 1].wait_recv()
            frm = lax.rem(me_f - o + n_freq, n_freq)
            out_ref[term, peer_rows(frm), :] = ag_got[term, o - 1].astype(F32)
    for move in moves + sums[0] + sums[1] + gathers[0] + gathers[1]:
        move.wait_send()


def body(visibilities, coords, vis_counts, cover_tile, offsets, channel, taper):
    n_span = lax.axis_size("span")
    n_freq = lax.axis_size("freq")
    sub = visibilities.shape[1]
    kk = visibilities.shape[-1]
    cap = max(4, 2 * sub // n_span)
    rows_per = -(-2 * TILE // (16 * n_freq)) * 16
    dma = pltpu.SemaphoreType.DMA
    block = cap * 16 + 16
    out = pl.pallas_call(
        functools.partial(kernel, n_span, n_freq, cap, rows_per),
        out_shape=jax.ShapeDtypeStruct((NT, n_freq * rows_per, 128), F32),
        in_specs=[pl.BlockSpec(memory_space=pltpu.VMEM)] * 7,
        out_specs=pl.BlockSpec(memory_space=pltpu.VMEM),
        scratch_shapes=[
            pltpu.VMEM((12, sub, kk), F32),
            pltpu.VMEM((14, sub, kk), F32),
            pltpu.VMEM((sub * 64, 256), BF16),
            pltpu.VMEM((sub * 64, 128), BF16),
            pltpu.VMEM((sub, 32, 128), F32),
            pltpu.VMEM((n_span, cap * 32, 256), BF16),
            pltpu.VMEM((8, 128), jnp.int32),
            pltpu.SMEM((8, 128), jnp.int32),
            pltpu.VMEM((n_span, block, 128), BF16),
            pltpu.VMEM((n_span - 1, block, 128), BF16),
            pltpu.VMEM((NT, n_freq * rows_per, 128), F32),
            pltpu.VMEM((NT, n_freq * rows_per, 128), BF16),
            pltpu.VMEM((NT, n_freq - 1, rows_per, 128), BF16),
            pltpu.VMEM((NT, rows_per, 128), BF16),
            pltpu.VMEM((NT, n_freq - 1, rows_per, 128), BF16),
            dma(()),
            dma((n_span - 1,)), dma((n_span - 1,)),
            dma((NT, n_freq - 1)), dma((NT, n_freq - 1)),
            dma((NT, n_freq - 1)), dma((NT, n_freq - 1)),
        ],
        compiler_params=pltpu.CompilerParams(
            collective_id=0, has_side_effects=True, vmem_limit_bytes=32 * 1024 * 1024
        ),
    )(
        cover_tile[:, :, 0], offsets[0].T, channel, vis_counts, coords[0], visibilities[0], taper,
    )
    return out[:, :2 * TILE].reshape(NT, 1, 2, TILE, TILE)


def solution(mesh):
    return jax.shard_map(
        body,
        mesh=mesh,
        in_specs=(
            P("freq", "span", None, None),
            P("freq", "span", None, None),
            P("freq", "span"),
            P("freq", "span", None),
            P("freq", "span", None),
            P("freq", "span"),
            P(),
        ),
        out_specs=P(None, "span", None, None, None),
        check_vma=False,
    )
```

```python
import functools
import math

import jax
import jax.numpy as jnp
from jax import lax
from jax.experimental import pallas as pl
from jax.experimental.pallas import tpu as pltpu
from jax.sharding import PartitionSpec as P

TILE = 128
NT = 2
CH_DEV = 16
SUB = 32
MESH = pl.DeviceIdType.MESH
F32 = jnp.float32
BF16 = jnp.bfloat16


def iota(shape, axis):
    return lax.broadcasted_iota(jnp.int32, shape, axis)


def unit_phase(turns):
    frac = turns - jnp.round(turns)
    half = frac * math.pi
    sq = half * half
    sin_h = sum_poly(sq, [(-1.0) ** n / math.factorial(2 * n + 1) for n in range(7)]) * half
    cos_h = sum_poly(sq, [(-1.0) ** n / math.factorial(2 * n) for n in range(8)])
    return 1.0 - 2.0 * sin_h * sin_h, 2.0 * sin_h * cos_h


def sum_poly(x, coefs):
    total = jnp.full_like(x, coefs[-1])
    for coef in coefs[-2::-1]:
        total = total * x + coef
    return total


def cmul(a, b):
    return a[0] * b[0] - a[1] * b[1], a[0] * b[1] + a[1] * b[0]


def kernel(
    n_span, n_freq, cap, rows_per, tile_ref, offs_ref, chan_ref, count_ref, coord_ref, vis_ref,
    taper_ref, out_ref, tile_v, offs_v, chan_v, count_v, coord_v, vis_v, taper_v, in_sem, ea, eb,
    ab_scr, g_scr, y_scr, z_scr, rhs_scr, src_v, src_s, send, got, acc_scr,
    rs_send, rs_got, src_sem, a_send, a_recv, r_send, r_recv, g_send, g_recv,
):
    me_s, me_f = lax.axis_index("span"), lax.axis_index("freq")
    barrier = pltpu.get_barrier_semaphore()
    for o in range(1, n_span):
        pl.semaphore_signal(
            barrier, inc=1, device_id=(lax.rem(me_s + o, n_span), me_f), device_id_type=MESH
        )
    for o in range(1, n_freq):
        pl.semaphore_signal(
            barrier, inc=1, device_id=(me_s, lax.rem(me_f + o, n_freq)), device_id_type=MESH
        )

    hbm = [tile_ref, offs_ref, chan_ref, count_ref, coord_ref, vis_ref, taper_ref]
    vmem = [tile_v, offs_v, chan_v, count_v, coord_v, vis_v, taper_v]
    fetch = [
        pltpu.make_async_copy(a, b, in_sem.at[n]) for n, (a, b) in enumerate(zip(hbm, vmem))
    ]
    for copy in fetch:
        copy.start()
    for copy in fetch[:4]:
        copy.wait()
    tile_ref, offs_ref, chan_ref, count_ref, coord_ref, vis_ref, taper_ref = vmem
    kk = coord_ref.shape[2]
    lanes = cap * 32
    data_rows = cap * 16
    slots = n_span * cap

    tile_l, chan_l = tile_ref[...].astype(F32), chan_ref[...].astype(F32)
    row_l, col_l = offs_ref[0:1, :].astype(F32), offs_ref[1:2, :].astype(F32)
    count_l = count_ref[...].astype(F32)
    kind = lax.rem(iota((16, SUB), 0), 4)
    meta = jnp.where(
        kind == 0, jnp.broadcast_to(row_l, (16, SUB)),
        jnp.where(kind == 1, 1.0, jnp.broadcast_to(chan_l, (16, SUB))),
    )
    eye = iota((SUB, SUB), 0) == iota((SUB, SUB), 1)

    def to_rows(row):
        return jnp.sum(
            jnp.where(eye, jnp.broadcast_to(row, (SUB, SUB)), 0.0), axis=1, keepdims=True
        )

    dest_l = tile_l
    dest_s = to_rows(dest_l)
    same = jnp.broadcast_to(dest_l, (SUB, SUB)) == dest_s
    lower = iota((SUB, SUB), 1) < iota((SUB, SUB), 0)
    upper = iota((SUB, SUB), 0) < iota((SUB, SUB), 1)
    rank_s = jnp.sum(jnp.where(same & lower, 1.0, 0.0), axis=1, keepdims=True)
    rank_l = jnp.sum(jnp.where(same & upper, 1.0, 0.0), axis=0, keepdims=True)
    slot_s = (dest_s * cap + rank_s).astype(jnp.int32)
    slot_l = (dest_l * cap + rank_l).astype(jnp.int32)
    hot = jnp.broadcast_to(slot_s, (SUB, 128)) == iota((SUB, 128), 1)
    src = jnp.sum(jnp.where(hot, iota((SUB, 128), 0).astype(F32), 0.0), axis=0, keepdims=True)
    turn_s = to_rows(col_l)
    turn_s = turn_s - 32.0 * jnp.floor(turn_s * (1.0 / 32.0))
    turn = jnp.sum(
        jnp.where(iota((SUB, 128), 0) == iota((SUB, 128), 1), turn_s, 0.0), axis=0, keepdims=True
    )
    src_v[...] = jnp.where(
        iota((8, 128), 0) == 0, jnp.broadcast_to(src, (8, 128)), jnp.broadcast_to(turn, (8, 128))
    ).astype(jnp.int32)
    src_copy = pltpu.make_async_copy(src_v, src_s, src_sem)
    src_copy.start()
    col_s = to_rows(col_l)
    count_s = to_rows(count_l)
    hot_t = jnp.broadcast_to(slot_l, (slots, SUB)) == iota((slots, SUB), 0)
    col_splat = jnp.dot(
        jnp.where(hot_t, 1.0, 0.0).astype(BF16),
        jnp.broadcast_to(col_s, (SUB, 128)).astype(BF16),
        preferred_element_type=F32,
    )
    hot_x = jnp.broadcast_to(slot_s, (SUB, slots * 32)) == iota((SUB, slots * 32), 1) // 32
    spread_meta = jnp.dot(
        meta.astype(BF16), jnp.where(hot_x, 1.0, 0.0).astype(BF16), preferred_element_type=F32
    )
    eight = iota((8, 128), 0)
    for d in range(n_span):
        cols = col_splat[d * cap:(d + 1) * cap]
        if cap < 8:
            cols = jnp.concatenate([cols, jnp.zeros((8 - cap, 128), F32)], 0)
        info = spread_meta[0:8, d * lanes:d * lanes + 128]
        if lanes > 128:
            info = jnp.where(eight < 4, info, spread_meta[0:8, d * lanes + 128:d * lanes + 256])
        send[d, data_rows:, :] = jnp.concatenate([cols, info], 0).astype(BF16)

    def powers(turns):
        e1 = unit_phase(turns)
        e2 = cmul(e1, e1)
        e3 = cmul(e2, e1)
        e4 = cmul(e2, e2)
        e8 = cmul(e4, e4)
        e16 = cmul(e8, e8)
        return e1, e2, e3, e4, e8, e16

    for copy in fetch[4:]:
        copy.wait()
    piece_lane = iota((8, 128), 1).astype(F32)
    for g in range(SUB // 8):
        rows = slice(8 * g, 8 * g + 8)
        left_over = jnp.broadcast_to(count_s[rows], (8, 128)) - piece_lane
        for kt in range(kk // 128):
            cols = slice(128 * kt, 128 * kt + 128)
            for n, val in enumerate(powers(coord_ref[rows, 0, cols] * (-1.0 / 32.0))):
                ea[rows, 8 * n + kt, :] = val[0]
                ea[rows, 8 * n + 4 + kt, :] = val[1]
            e1, e2, e3, e4, e8, e16 = powers(coord_ref[rows, 1, cols] * (-1.0 / 32.0))
            live = jnp.where(left_over > 128.0 * kt, 1.0 / math.sqrt(kk), 0.0)
            vis = vis_ref[rows, :, cols].astype(F32)
            w0 = (vis[:, 0, :] * live, vis[:, 1, :] * live)
            for n, val in enumerate([w0, cmul(w0, e1), cmul(w0, e2), cmul(w0, e3), e4, e8, e16]):
                eb[rows, 8 * n + kt, :] = val[0]
                eb[rows, 8 * n + 4 + kt, :] = val[1]

    sub8 = iota((8, 128), 0)
    bit0, bit1, bit2 = lax.rem(sub8, 2) == 1, lax.rem(sub8 // 2, 2) == 1, sub8 >= 4
    taper = taper_ref[...]
    taper = jnp.concatenate([taper, taper], 1)
    taper = jnp.concatenate([taper, taper], 0)
    taper = jnp.concatenate([taper, taper], 1)
    low_half64 = iota((64, 128), 1) < 64

    def expand(rows4, e4, e8, e16):
        low = [
            jnp.where(
                bit1, jnp.where(bit0, rows4[3][c], rows4[2][c]),
                jnp.where(bit0, rows4[1][c], rows4[0][c]),
            )
            for c in range(2)
        ]
        base = cmul(low, (jnp.where(bit2, e4[0], 1.0), jnp.where(bit2, e4[1], 0.0)))
        rr, ii = base[0] * e8[0], base[1] * e8[1]
        ri, ir = base[0] * e8[1], base[1] * e8[0]
        first = (base[0] * e16[0] + base[1] * e16[1], base[1] * e16[0] - base[0] * e16[1])
        blocks = [first, (rr + ii, ir - ri), base, (rr - ii, ri + ir)]
        return [
            jnp.concatenate([blocks[2 * half][c], blocks[2 * half + 1][c]], 0).astype(BF16)
            for c in range(2) for half in range(2)
        ]

    group = 8

    def sub_group(i, carry):
        for u in range(group):
            s = i * group + u
            for kt in range(kk // 128):
                cols = slice(128 * kt, 128 * kt + 128)

                def row(ref, n):
                    return tuple(
                        jnp.broadcast_to(ref[s, at:at + 1, :], (8, 128))
                        for at in (8 * n + kt, 8 * n + 4 + kt)
                    )

                one = (jnp.ones((8, 128), F32), jnp.zeros((8, 128), F32))
                a_rows = expand(
                    [one] + [row(ea, n) for n in range(3)], *[row(ea, n) for n in range(3, 6)]
                )
                b_rows = expand(
                    [row(eb, n) for n in range(4)], *[row(eb, n) for n in range(4, 7)]
                )
                for n in range(4):
                    ab_scr[u, 0, 16 * n:16 * n + 16, cols] = a_rows[n]
                    ab_scr[u, 1, 16 * n:16 * n + 16, cols] = b_rows[n]
            grid = lax.dot_general(
                ab_scr[u, 0], ab_scr[u, 1], (((1,), (1,)), ((), ())), preferred_element_type=F32
            )
            wide = jnp.concatenate([grid, grid], 1) * taper
            high = wide.astype(BF16)
            rest = (wide - high.astype(F32)).astype(BF16)
            rows = pl.ds(pl.multiple_of(s * 64, 64), 64)
            g_scr[rows, 0:128] = high
            g_scr[rows, 128:256] = rest
        return carry

    lax.fori_loop(0, SUB // group, sub_group, 0)

    def turns_of(rows, cols):
        prod = (lax.rem(rows, 32) - 16) * (lax.rem(cols, 32) - 16)
        return prod.astype(F32) * (-1.0 / 32.0)

    def quarter(n):
        return n.astype(F32) * 0.25

    rows, cols = iota((64, 128), 0), iota((64, 128), 1)
    right = unit_phase(
        turns_of(rows, cols) + quarter(cols // 64 + rows // 32 - lax.rem(cols // 32, 2))
    )[0]
    right_h = right.astype(BF16)
    right_l = (right - right_h.astype(F32)).astype(BF16)
    right = jnp.concatenate([right_h, right_l, right_h, jnp.zeros((64, 128), BF16)], 0)
    rows, cols = iota((64, 64), 0), iota((64, 64), 1)
    left = unit_phase(turns_of(rows, cols) + quarter(cols // 32 - rows // 32))[0]
    left = (left * (1.0 / 32.0)).astype(BF16)
    rows, cols = iota((128, 512), 0), iota((128, 512), 1)
    repeat = jnp.where(
        (rows // 32 == cols // 128) & (lax.rem(rows, 32) == lax.rem(cols, 32)), 1.0, 0.0
    ).astype(BF16)

    y_scr[...] = jnp.dot(g_scr[...], right, preferred_element_type=F32).astype(BF16)
    lane32 = lax.rem(iota((32, 128), 1), 32)
    src_copy.wait()

    def second(s, carry):
        part = jnp.dot(
            left, y_scr[pl.ds(pl.multiple_of(s * 64, 64), 64), :], preferred_element_type=F32
        )
        sub = part[:32] + pltpu.roll(part[32:], 64, 1)
        turn = jnp.clip(src_s[1, s], 0, 31)
        z_scr[s] = jnp.where(
            lane32 >= turn, pltpu.roll(sub, turn, 1), pltpu.roll(sub, turn + 96, 1)
        )
        return carry

    lax.fori_loop(0, SUB, second, 0, unroll=16)

    low_half = iota((32, 128), 1) < 64
    for pair in range(slots // 2):
        left_z = z_scr[jnp.clip(src_s[0, 2 * pair], 0, SUB - 1)]
        right_z = pltpu.roll(z_scr[jnp.clip(src_s[0, 2 * pair + 1], 0, SUB - 1)], 64, 1)
        d, j = pair // (cap // 2), pair % (cap // 2)
        send[d, 32 * j:32 * j + 32, :] = jnp.where(low_half, left_z, right_z).astype(BF16)

    pl.semaphore_wait(barrier, n_span + n_freq - 2)
    moves = []
    for o in range(1, n_span):
        to = lax.rem(me_s + o, n_span)
        move = pltpu.make_async_remote_copy(
            src_ref=send.at[to], dst_ref=got.at[o - 1], send_sem=a_send.at[o - 1],
            recv_sem=a_recv.at[o - 1], device_id=(to, me_f), device_id_type=MESH,
        )
        move.start()
        moves.append(move)

    channels = CH_DEV * n_freq
    lane = iota((1, 128), 1)
    lane_a = lax.rem(lane, 32).astype(F32)
    cell_row = iota((TILE, 128), 0).astype(F32)

    def widen(block, n):
        wide = jnp.dot(block[0:data_rows, :], repeat, preferred_element_type=F32)
        info = block[data_rows:, :].astype(F32)
        for i in range(cap):
            j, h = i // 2, i % 2
            off = piece_lane - jnp.broadcast_to(info[i:i + 1, :], (8, 128))
            inside = jnp.where((off >= 0.0) & (off < 32.0), 1.0, 0.0)
            inside = jnp.concatenate([inside] * 4, 0) > 0.5
            part = wide[32 * j:32 * j + 32, 256 * h:256 * h + 256]
            rhs_scr[n, 32 * i:32 * i + 32, 0:128] = jnp.where(
                inside, part[:, :128], 0.0
            ).astype(BF16)
            rhs_scr[n, 32 * i:32 * i + 32, 128:256] = jnp.where(
                inside, part[:, 128:], 0.0
            ).astype(BF16)

    exact = channels & (channels - 1) == 0 and channels <= 256

    def weigh(block, n, term):
        info = block[data_rows:, :].astype(F32)
        high, low = [], []
        for j in range(lanes // 128):
            at = 8 + 4 * j
            hit = cell_row == info[at:at + 1, :] + lane_a
            val = info[at + 1:at + 2, :]
            if term == 1:
                chan = info[at + 2:at + 3, :] + (me_f * CH_DEV).astype(F32)
                val = val * ((2.0 * chan + 1.0 - channels) / channels)
            cut = val.astype(BF16).astype(F32)
            high.append(jnp.where(hit, jnp.broadcast_to(cut, (TILE, 128)), 0.0).astype(BF16))
            low.append(jnp.where(hit, jnp.broadcast_to(val - cut, (TILE, 128)), 0.0).astype(BF16))
        res = jnp.dot(jnp.concatenate(high, 1), rhs_scr[n], preferred_element_type=F32)
        if term == 1 and not exact:
            res = res + jnp.dot(jnp.concatenate(low, 1), rhs_scr[n], preferred_element_type=F32)
        return res

    blocks = [send.at[me_s]] + [got.at[o - 1] for o in range(1, n_span)]
    acc = None
    starts = [0, 1, n_span // 2, n_span]
    for first, last in zip(starts[:-1], starts[1:]):
        for n in range(first, last):
            if n:
                moves[n - 1].wait_recv()
        for n in range(first, last):
            widen(blocks[n], n)
        for n in range(first, last):
            res = weigh(blocks[n], n, 0)
            acc = res if acc is None else acc + res

    def peer_rows(place):
        return pl.ds(pl.multiple_of(place * rows_per, rows_per), rows_per)

    half = 2 * TILE
    pad = n_freq * rows_per - half

    def scatter(acc, term):
        if pad:
            acc_scr[term, half:, :] = jnp.zeros((pad, 128), F32)
            rs_send[term, half:, :] = jnp.zeros((pad, 128), BF16)
        for c in range(2):
            part = acc[:, c * 128:(c + 1) * 128]
            acc_scr[term, c * TILE:(c + 1) * TILE, :] = part
            rs_send[term, c * TILE:(c + 1) * TILE, :] = part.astype(BF16)
        started = []
        for o in range(1, n_freq):
            to = lax.rem(me_f + o, n_freq)
            move = pltpu.make_async_remote_copy(
                src_ref=rs_send.at[term, peer_rows(to)], dst_ref=rs_got.at[term, o - 1],
                send_sem=r_send.at[term, o - 1], recv_sem=r_recv.at[term, o - 1],
                device_id=(me_s, to), device_id_type=MESH,
            )
            move.start()
            started.append(move)
        return started

    sums = [scatter(acc, 0)]
    acc = None
    for n, block in enumerate(blocks):
        res = weigh(block, n, 1)
        acc = res if acc is None else acc + res
    sums.append(scatter(acc, 1))

    scale = TILE / (32.0 * math.sqrt(n_freq * SUB))
    gathers = []
    for term in range(NT):
        total = acc_scr[term, peer_rows(me_f), :]
        for o in range(1, n_freq):
            sums[term][o - 1].wait_recv()
            total = total + rs_got[term, o - 1].astype(F32)
        mine = out_ref.at[term, peer_rows(me_f)]
        mine[...] = (total * scale).astype(BF16)
        started = []
        for o in range(1, n_freq):
            to = lax.rem(me_f + o, n_freq)
            move = pltpu.make_async_remote_copy(
                src_ref=mine, dst_ref=mine,
                send_sem=g_send.at[term, o - 1], recv_sem=g_recv.at[term, o - 1],
                device_id=(me_s, to), device_id_type=MESH,
            )
            move.start()
            started.append(move)
        gathers.append(started)
    for term in range(NT):
        for o in range(1, n_freq):
            gathers[term][o - 1].wait_recv()
    for move in moves + sums[0] + sums[1] + gathers[0] + gathers[1]:
        move.wait_send()


def body(visibilities, coords, vis_counts, cover_tile, offsets, channel, taper):
    n_span = lax.axis_size("span")
    n_freq = lax.axis_size("freq")
    sub = visibilities.shape[1]
    kk = visibilities.shape[-1]
    cap = max(4, 2 * sub // n_span)
    rows_per = -(-2 * TILE // (16 * n_freq)) * 16
    dma = pltpu.SemaphoreType.DMA
    block = cap * 16 + 16
    out = pl.pallas_call(
        functools.partial(kernel, n_span, n_freq, cap, rows_per),
        out_shape=jax.ShapeDtypeStruct((NT, n_freq * rows_per, 128), BF16),
        in_specs=[pl.BlockSpec(memory_space=pltpu.HBM)] * 7,
        out_specs=pl.BlockSpec(memory_space=pltpu.VMEM),
        scratch_shapes=[
            pltpu.VMEM((1, sub), jnp.int32),
            pltpu.VMEM((2, sub), jnp.int32),
            pltpu.VMEM((1, sub), jnp.int32),
            pltpu.VMEM((1, sub), jnp.int32),
            pltpu.VMEM((sub, 2, kk), F32),
            pltpu.VMEM((sub, 2, kk), BF16),
            pltpu.VMEM((32, 32), F32),
            dma((7,)),
            pltpu.VMEM((sub, 48, 128), F32),
            pltpu.VMEM((sub, 56, 128), F32),
            pltpu.VMEM((8, 2, 64, kk), BF16),
            pltpu.VMEM((sub * 64, 256), BF16),
            pltpu.VMEM((sub * 64, 128), BF16),
            pltpu.VMEM((sub, 32, 128), F32),
            pltpu.VMEM((n_span, cap * 32, 256), BF16),
            pltpu.VMEM((8, 128), jnp.int32),
            pltpu.SMEM((8, 128), jnp.int32),
            pltpu.VMEM((n_span, block, 128), BF16),
            pltpu.VMEM((n_span - 1, block, 128), BF16),
            pltpu.VMEM((NT, n_freq * rows_per, 128), F32),
            pltpu.VMEM((NT, n_freq * rows_per, 128), BF16),
            pltpu.VMEM((NT, n_freq - 1, rows_per, 128), BF16),
            dma(()),
            dma((n_span - 1,)), dma((n_span - 1,)),
            dma((NT, n_freq - 1)), dma((NT, n_freq - 1)),
            dma((NT, n_freq - 1)), dma((NT, n_freq - 1)),
        ],
        compiler_params=pltpu.CompilerParams(
            collective_id=0, has_side_effects=True, vmem_limit_bytes=60 * 1024 * 1024
        ),
    )(
        cover_tile[:, :, 0], offsets[0].T, channel, vis_counts, coords[0], visibilities[0], taper,
    )
    return out[:, :2 * TILE].astype(F32).reshape(NT, 1, 2, TILE, TILE)


def solution(mesh):
    return jax.shard_map(
        body,
        mesh=mesh,
        in_specs=(
            P("freq", "span", None, None),
            P("freq", "span", None, None),
            P("freq", "span"),
            P("freq", "span", None),
            P("freq", "span", None),
            P("freq", "span"),
            P(),
        ),
        out_specs=P(None, "span", None, None, None),
        check_vma=False,
    )
```

```python
import functools
import math

import jax
import jax.numpy as jnp
from jax import lax
from jax.experimental import pallas as pl
from jax.experimental.pallas import tpu as pltpu
from jax.sharding import PartitionSpec as P

TILE = 128
NT = 2
CH_DEV = 16
SUB = 32
MESH = pl.DeviceIdType.MESH
F32 = jnp.float32
BF16 = jnp.bfloat16


def iota(shape, axis):
    return lax.broadcasted_iota(jnp.int32, shape, axis)


def unit_phase(turns):
    frac = turns - jnp.round(turns)
    half = frac * math.pi
    sq = half * half
    sin_h = sum_poly(sq, [(-1.0) ** n / math.factorial(2 * n + 1) for n in range(7)]) * half
    cos_h = sum_poly(sq, [(-1.0) ** n / math.factorial(2 * n) for n in range(8)])
    return 1.0 - 2.0 * sin_h * sin_h, 2.0 * sin_h * cos_h


def sum_poly(x, coefs):
    total = jnp.full_like(x, coefs[-1])
    for coef in coefs[-2::-1]:
        total = total * x + coef
    return total


def cmul(a, b):
    return a[0] * b[0] - a[1] * b[1], a[0] * b[1] + a[1] * b[0]


def kernel(
    n_span, n_freq, cap, rows_per, tile_ref, offs_ref, chan_ref, count_ref, coord_ref, vis_ref,
    taper_ref, out_ref, tile_v, offs_v, chan_v, count_v, coord_v, vis_v, taper_v, in_sem, ea, eb,
    ab_scr, g_scr, y_scr, z_scr, rhs_scr, src_v, src_s, send, got, tile_scr, count_scr, acc_scr,
    rs_send, rs_got, src_sem, a_send, a_recv, r_send, r_recv, g_send, g_recv,
):
    me_s, me_f = lax.axis_index("span"), lax.axis_index("freq")
    barrier = pltpu.get_barrier_semaphore()
    for o in range(1, n_span):
        pl.semaphore_signal(
            barrier, inc=1, device_id=(lax.rem(me_s + o, n_span), me_f), device_id_type=MESH
        )
    for o in range(1, n_freq):
        pl.semaphore_signal(
            barrier, inc=1, device_id=(me_s, lax.rem(me_f + o, n_freq)), device_id_type=MESH
        )

    hbm = [tile_ref, offs_ref, chan_ref, count_ref, coord_ref, vis_ref, taper_ref]
    vmem = [tile_v, offs_v, chan_v, count_v, coord_v, vis_v, taper_v]
    fetch = [
        pltpu.make_async_copy(a, b, in_sem.at[n]) for n, (a, b) in enumerate(zip(hbm, vmem))
    ]
    for copy in fetch:
        copy.start()
    for copy in fetch[:4]:
        copy.wait()
    tile_ref, offs_ref, chan_ref, count_ref, coord_ref, vis_ref, taper_ref = vmem
    kk = coord_ref.shape[2]
    lanes = cap * 32
    data_rows = cap * 16
    slots = n_span * cap

    tile_l, chan_l = tile_ref[...].astype(F32), chan_ref[...].astype(F32)
    row_l, col_l = offs_ref[0:1, :].astype(F32), offs_ref[1:2, :].astype(F32)
    count_l = count_ref[...].astype(F32)
    kind = iota((16, SUB), 0) & 3
    meta = jnp.where(
        kind == 0, jnp.broadcast_to(row_l, (16, SUB)),
        jnp.where(kind == 1, 1.0, jnp.broadcast_to(chan_l, (16, SUB))),
    )
    eye = iota((SUB, SUB), 0) == iota((SUB, SUB), 1)

    def to_rows(row):
        return jnp.sum(
            jnp.where(eye, jnp.broadcast_to(row, (SUB, SUB)), 0.0), axis=1, keepdims=True
        )

    dest_l = tile_l
    dest_s = to_rows(dest_l)
    same = jnp.broadcast_to(dest_l, (SUB, SUB)) == dest_s
    lower = iota((SUB, SUB), 1) < iota((SUB, SUB), 0)
    upper = iota((SUB, SUB), 0) < iota((SUB, SUB), 1)
    rank_s = jnp.sum(jnp.where(same & lower, 1.0, 0.0), axis=1, keepdims=True)
    rank_l = jnp.sum(jnp.where(same & upper, 1.0, 0.0), axis=0, keepdims=True)
    slot_s = (dest_s * cap + rank_s).astype(jnp.int32)
    slot_l = (dest_l * cap + rank_l).astype(jnp.int32)
    hot = jnp.broadcast_to(slot_s, (SUB, 128)) == iota((SUB, 128), 1)
    src = jnp.sum(jnp.where(hot, iota((SUB, 128), 0).astype(F32), 0.0), axis=0, keepdims=True)
    turn_s = to_rows(col_l)
    turn_s = turn_s - 32.0 * jnp.floor(turn_s * (1.0 / 32.0))
    turn = jnp.sum(
        jnp.where(iota((SUB, 128), 0) == iota((SUB, 128), 1), turn_s, 0.0), axis=0, keepdims=True
    )
    src_v[...] = jnp.where(
        iota((8, 128), 0) == 0, jnp.broadcast_to(src, (8, 128)), jnp.broadcast_to(turn, (8, 128))
    ).astype(jnp.int32)
    src_copy = pltpu.make_async_copy(src_v, src_s, src_sem)
    src_copy.start()
    col_s = to_rows(col_l)
    count_s = to_rows(count_l)
    hot_t = jnp.broadcast_to(slot_l, (slots, SUB)) == iota((slots, SUB), 0)
    col_splat = jnp.dot(
        jnp.where(hot_t, 1.0, 0.0).astype(BF16),
        jnp.broadcast_to(col_s, (SUB, 128)).astype(BF16),
        preferred_element_type=F32,
    )
    hot_x = jnp.broadcast_to(slot_s, (SUB, slots * 32)) == iota((SUB, slots * 32), 1) >> 5
    spread_meta = jnp.dot(
        meta.astype(BF16), jnp.where(hot_x, 1.0, 0.0).astype(BF16), preferred_element_type=F32
    )
    eight = iota((8, 128), 0)
    for d in range(n_span):
        cols = col_splat[d * cap:(d + 1) * cap]
        if cap < 8:
            cols = jnp.concatenate([cols, jnp.zeros((8 - cap, 128), F32)], 0)
        info = spread_meta[0:8, d * lanes:d * lanes + 128]
        if lanes > 128:
            info = jnp.where(eight < 4, info, spread_meta[0:8, d * lanes + 128:d * lanes + 256])
        send[d, data_rows:, :] = jnp.concatenate([cols, info], 0).astype(BF16)

    def powers(turns):
        e1 = unit_phase(turns)
        e2 = cmul(e1, e1)
        e3 = cmul(e2, e1)
        e4 = cmul(e2, e2)
        e8 = cmul(e4, e4)
        e16 = cmul(e8, e8)
        return e1, e2, e3, e4, e8, e16

    for copy in fetch[4:]:
        copy.wait()
    piece_lane = iota((8, 128), 1).astype(F32)
    count_scr[...] = jnp.broadcast_to(count_s, (SUB, 128))

    def phases(g, carry):
        rows = pl.ds(pl.multiple_of(g * 8, 8), 8)
        left_over = count_scr[rows, :] - piece_lane
        for kt in range(kk // 128):
            cols = slice(128 * kt, 128 * kt + 128)
            for n, val in enumerate(powers(coord_ref[rows, 0, cols] * (-1.0 / 32.0))):
                ea[rows, 8 * n + kt, :] = val[0]
                ea[rows, 8 * n + 4 + kt, :] = val[1]
            e1, e2, e3, e4, e8, e16 = powers(coord_ref[rows, 1, cols] * (-1.0 / 32.0))
            live = jnp.where(left_over > 128.0 * kt, 1.0 / math.sqrt(kk), 0.0)
            vis = vis_ref[rows, :, cols].astype(F32)
            w0 = (vis[:, 0, :] * live, vis[:, 1, :] * live)
            for n, val in enumerate([w0, cmul(w0, e1), cmul(w0, e2), cmul(w0, e3), e4, e8, e16]):
                eb[rows, 8 * n + kt, :] = val[0]
                eb[rows, 8 * n + 4 + kt, :] = val[1]
        return carry

    lax.fori_loop(0, SUB // 8, phases, 0)

    sub8 = iota((8, 128), 0)
    bit0, bit1, bit2 = (sub8 & 1) == 1, (sub8 & 2) == 2, sub8 >= 4
    taper = taper_ref[...]
    taper = jnp.concatenate([taper, taper], 1)
    taper = jnp.concatenate([taper, taper], 0)
    taper = jnp.concatenate([taper, taper], 1)
    low_half64 = iota((64, 128), 1) < 64

    def expand(rows4, e4, e8, e16):
        low = [
            jnp.where(
                bit1, jnp.where(bit0, rows4[3][c], rows4[2][c]),
                jnp.where(bit0, rows4[1][c], rows4[0][c]),
            )
            for c in range(2)
        ]
        base = cmul(low, (jnp.where(bit2, e4[0], 1.0), jnp.where(bit2, e4[1], 0.0)))
        rr, ii = base[0] * e8[0], base[1] * e8[1]
        ri, ir = base[0] * e8[1], base[1] * e8[0]
        first = (base[0] * e16[0] + base[1] * e16[1], base[1] * e16[0] - base[0] * e16[1])
        blocks = [first, (rr + ii, ir - ri), base, (rr - ii, ri + ir)]
        return [
            jnp.concatenate([blocks[2 * half][c], blocks[2 * half + 1][c]], 0).astype(BF16)
            for c in range(2) for half in range(2)
        ]

    group = 4

    def sub_group(i, carry):
        for u in range(group):
            s = i * group + u
            for kt in range(kk // 128):
                cols = slice(128 * kt, 128 * kt + 128)

                def row(ref, n):
                    return tuple(
                        jnp.broadcast_to(ref[s, at:at + 1, :], (8, 128))
                        for at in (8 * n + kt, 8 * n + 4 + kt)
                    )

                one = (jnp.ones((8, 128), F32), jnp.zeros((8, 128), F32))
                a_rows = expand(
                    [one] + [row(ea, n) for n in range(3)], *[row(ea, n) for n in range(3, 6)]
                )
                b_rows = expand(
                    [row(eb, n) for n in range(4)], *[row(eb, n) for n in range(4, 7)]
                )
                for n in range(4):
                    ab_scr[u, 0, 16 * n:16 * n + 16, cols] = a_rows[n]
                    ab_scr[u, 1, 16 * n:16 * n + 16, cols] = b_rows[n]
            grid = lax.dot_general(
                ab_scr[u, 0], ab_scr[u, 1], (((1,), (1,)), ((), ())), preferred_element_type=F32
            )
            wide = jnp.concatenate([grid, grid], 1) * taper
            high = wide.astype(BF16)
            rest = (wide - high.astype(F32)).astype(BF16)
            rows = pl.ds(pl.multiple_of(s * 64, 64), 64)
            g_scr[rows, 0:128] = high
            g_scr[rows, 128:256] = rest
        return carry

    lax.fori_loop(0, SUB // group, sub_group, 0)

    def turns_of(rows, cols):
        prod = ((rows & 31) - 16) * ((cols & 31) - 16)
        return prod.astype(F32) * (-1.0 / 32.0)

    def quarter(n):
        return n.astype(F32) * 0.25

    rows, cols = iota((64, 128), 0), iota((64, 128), 1)
    right = unit_phase(
        turns_of(rows, cols) + quarter((cols >> 6) + (rows >> 5) - ((cols >> 5) & 1))
    )[0]
    right_h = right.astype(BF16)
    right_l = (right - right_h.astype(F32)).astype(BF16)
    right = jnp.concatenate([right_h, right_l, right_h, jnp.zeros((64, 128), BF16)], 0)
    rows, cols = iota((64, 64), 0), iota((64, 64), 1)
    left = unit_phase(turns_of(rows, cols) + quarter((cols >> 5) - (rows >> 5)))[0]
    left = (left * (1.0 / 32.0)).astype(BF16)
    rows, cols = iota((128, 512), 0), iota((128, 512), 1)
    repeat = jnp.where(
        ((rows >> 5) == (cols >> 7)) & ((rows & 31) == (cols & 31)), 1.0, 0.0
    ).astype(BF16)

    y_scr[...] = jnp.dot(g_scr[...], right, preferred_element_type=F32).astype(BF16)
    lane32 = iota((32, 128), 1) & 31
    src_copy.wait()

    def second(s, carry):
        part = jnp.dot(
            left, y_scr[pl.ds(pl.multiple_of(s * 64, 64), 64), :], preferred_element_type=F32
        )
        sub = part[:32] + pltpu.roll(part[32:], 64, 1)
        turn = jnp.clip(src_s[1, s], 0, 31)
        z_scr[s] = jnp.where(
            lane32 >= turn, pltpu.roll(sub, turn, 1), pltpu.roll(sub, turn + 96, 1)
        )
        return carry

    lax.fori_loop(0, SUB, second, 0, unroll=8)

    low_half = iota((32, 128), 1) < 64

    def fill(d, carry):
        for j in range(cap // 2):
            pair = d * (cap // 2) + j
            left_z = z_scr[jnp.clip(src_s[0, 2 * pair], 0, SUB - 1)]
            right_z = pltpu.roll(z_scr[jnp.clip(src_s[0, 2 * pair + 1], 0, SUB - 1)], 64, 1)
            send[d, 32 * j:32 * j + 32, :] = jnp.where(low_half, left_z, right_z).astype(BF16)
        return carry

    lax.fori_loop(0, n_span, fill, 0)

    pl.semaphore_wait(barrier, n_span + n_freq - 2)
    moves = []
    for o in range(1, n_span):
        to = lax.rem(me_s + o, n_span)
        move = pltpu.make_async_remote_copy(
            src_ref=send.at[to], dst_ref=got.at[o], send_sem=a_send.at[o],
            recv_sem=a_recv.at[o], device_id=(to, me_f), device_id_type=MESH,
        )
        move.start()
        moves.append(move)

    channels = CH_DEV * n_freq
    lane = iota((1, 128), 1)
    lane_a = (lane & 31).astype(F32)
    cell_row = iota((TILE, 128), 0).astype(F32)

    def widen(n):
        wide = jnp.dot(got[n, 0:data_rows, :], repeat, preferred_element_type=F32)
        info = got[n, data_rows:, :].astype(F32)
        for i in range(cap):
            j, h = i // 2, i % 2
            off = piece_lane - jnp.broadcast_to(info[i:i + 1, :], (8, 128))
            inside = jnp.where((off >= 0.0) & (off < 32.0), 1.0, 0.0)
            inside = jnp.concatenate([inside] * 4, 0)
            part = wide[32 * j:32 * j + 32, 256 * h:256 * h + 256]
            rhs_scr[n, 32 * i:32 * i + 32, 0:128] = (part[:, :128] * inside).astype(BF16)
            rhs_scr[n, 32 * i:32 * i + 32, 128:256] = (part[:, 128:] * inside).astype(BF16)

    exact = channels & (channels - 1) == 0 and channels <= 256

    def weigh(n, term):
        info = got[n, data_rows:, :].astype(F32)
        high, low = [], []
        for j in range(lanes // 128):
            at = 8 + 4 * j
            hit = cell_row == info[at:at + 1, :] + lane_a
            val = info[at + 1:at + 2, :]
            if term == 1:
                chan = info[at + 2:at + 3, :] + (me_f * CH_DEV).astype(F32)
                val = val * ((2.0 * chan + 1.0 - channels) / channels)
            cut = val.astype(BF16).astype(F32)
            high.append(jnp.where(hit, jnp.broadcast_to(cut, (TILE, 128)), 0.0).astype(BF16))
            low.append(jnp.where(hit, jnp.broadcast_to(val - cut, (TILE, 128)), 0.0).astype(BF16))
        res = jnp.dot(jnp.concatenate(high, 1), rhs_scr[n], preferred_element_type=F32)
        if term == 1 and not exact:
            res = res + jnp.dot(jnp.concatenate(low, 1), rhs_scr[n], preferred_element_type=F32)
        return res

    got[0] = send[me_s]
    widen(0)
    tile_scr[...] = weigh(0, 0)

    def receive(o, carry):
        pltpu.make_async_remote_copy(
            src_ref=send.at[0], dst_ref=got.at[o], send_sem=a_send.at[o], recv_sem=a_recv.at[o],
            device_id=(lax.rem(me_s + 1, n_span), me_f), device_id_type=MESH,
        ).wait_recv()
        widen(o)
        tile_scr[...] += weigh(o, 0)
        return carry

    lax.fori_loop(1, n_span, receive, 0)

    def peer_rows(place):
        return pl.ds(pl.multiple_of(place * rows_per, rows_per), rows_per)

    half = 2 * TILE
    pad = n_freq * rows_per - half

    def scatter(term):
        acc = tile_scr[...]
        if pad:
            acc_scr[term, half:, :] = jnp.zeros((pad, 128), F32)
            rs_send[term, half:, :] = jnp.zeros((pad, 128), BF16)
        for c in range(2):
            part = acc[:, c * 128:(c + 1) * 128]
            acc_scr[term, c * TILE:(c + 1) * TILE, :] = part
            rs_send[term, c * TILE:(c + 1) * TILE, :] = part.astype(BF16)
        started = []
        for o in range(1, n_freq):
            to = lax.rem(me_f + o, n_freq)
            move = pltpu.make_async_remote_copy(
                src_ref=rs_send.at[term, peer_rows(to)], dst_ref=rs_got.at[term, o - 1],
                send_sem=r_send.at[term, o - 1], recv_sem=r_recv.at[term, o - 1],
                device_id=(me_s, to), device_id_type=MESH,
            )
            move.start()
            started.append(move)
        return started

    sums = [scatter(0)]
    tile_scr[...] = weigh(0, 1)

    def second_term(o, carry):
        tile_scr[...] += weigh(o, 1)
        return carry

    lax.fori_loop(1, n_span, second_term, 0)
    sums.append(scatter(1))

    scale = TILE / (32.0 * math.sqrt(n_freq * SUB))
    gathers = []
    for term in range(NT):
        total = acc_scr[term, peer_rows(me_f), :]
        for o in range(1, n_freq):
            sums[term][o - 1].wait_recv()
            total = total + rs_got[term, o - 1].astype(F32)
        mine = out_ref.at[term, peer_rows(me_f)]
        mine[...] = (total * scale).astype(BF16)
        started = []
        for o in range(1, n_freq):
            to = lax.rem(me_f + o, n_freq)
            move = pltpu.make_async_remote_copy(
                src_ref=mine, dst_ref=mine,
                send_sem=g_send.at[term, o - 1], recv_sem=g_recv.at[term, o - 1],
                device_id=(me_s, to), device_id_type=MESH,
            )
            move.start()
            started.append(move)
        gathers.append(started)
    for term in range(NT):
        for o in range(1, n_freq):
            gathers[term][o - 1].wait_recv()
    for move in moves + sums[0] + sums[1] + gathers[0] + gathers[1]:
        move.wait_send()


def body(visibilities, coords, vis_counts, cover_tile, offsets, channel, taper):
    n_span = lax.axis_size("span")
    n_freq = lax.axis_size("freq")
    sub = visibilities.shape[1]
    kk = visibilities.shape[-1]
    cap = max(4, 2 * sub // n_span)
    rows_per = -(-2 * TILE // (16 * n_freq)) * 16
    dma = pltpu.SemaphoreType.DMA
    block = cap * 16 + 16
    out = pl.pallas_call(
        functools.partial(kernel, n_span, n_freq, cap, rows_per),
        out_shape=jax.ShapeDtypeStruct((NT, n_freq * rows_per, 128), BF16),
        in_specs=[pl.BlockSpec(memory_space=pltpu.HBM)] * 7,
        out_specs=pl.BlockSpec(memory_space=pltpu.VMEM),
        scratch_shapes=[
            pltpu.VMEM((1, sub), jnp.int32),
            pltpu.VMEM((2, sub), jnp.int32),
            pltpu.VMEM((1, sub), jnp.int32),
            pltpu.VMEM((1, sub), jnp.int32),
            pltpu.VMEM((sub, 2, kk), F32),
            pltpu.VMEM((sub, 2, kk), BF16),
            pltpu.VMEM((32, 32), F32),
            dma((7,)),
            pltpu.VMEM((sub, 48, 128), F32),
            pltpu.VMEM((sub, 56, 128), F32),
            pltpu.VMEM((4, 2, 64, kk), BF16),
            pltpu.VMEM((sub * 64, 256), BF16),
            pltpu.VMEM((sub * 64, 128), BF16),
            pltpu.VMEM((sub, 32, 128), F32),
            pltpu.VMEM((n_span, cap * 32, 256), BF16),
            pltpu.VMEM((8, 128), jnp.int32),
            pltpu.SMEM((8, 128), jnp.int32),
            pltpu.VMEM((n_span, block, 128), BF16),
            pltpu.VMEM((n_span, block, 128), BF16),
            pltpu.VMEM((TILE, 256), F32),
            pltpu.VMEM((sub, 128), F32),
            pltpu.VMEM((NT, n_freq * rows_per, 128), F32),
            pltpu.VMEM((NT, n_freq * rows_per, 128), BF16),
            pltpu.VMEM((NT, n_freq - 1, rows_per, 128), BF16),
            dma(()),
            dma((n_span,)), dma((n_span,)),
            dma((NT, n_freq - 1)), dma((NT, n_freq - 1)),
            dma((NT, n_freq - 1)), dma((NT, n_freq - 1)),
        ],
        compiler_params=pltpu.CompilerParams(
            collective_id=0, has_side_effects=True, vmem_limit_bytes=60 * 1024 * 1024
        ),
    )(
        cover_tile[:, :, 0], offsets[0].T, channel, vis_counts, coords[0], visibilities[0], taper,
    )
    return out[:, :2 * TILE].astype(F32).reshape(NT, 1, 2, TILE, TILE)


def solution(mesh):
    return jax.shard_map(
        body,
        mesh=mesh,
        in_specs=(
            P("freq", "span", None, None),
            P("freq", "span", None, None),
            P("freq", "span"),
            P("freq", "span", None),
            P("freq", "span", None),
            P("freq", "span"),
            P(),
        ),
        out_specs=P(None, "span", None, None, None),
        check_vma=False,
    )
```

```python
import functools
import math

import jax
import jax.numpy as jnp
from jax import lax
from jax.experimental import pallas as pl
from jax.experimental.pallas import tpu as pltpu
from jax.sharding import PartitionSpec as P

TILE = 128
NT = 2
CH_DEV = 16
SUB = 32
MESH = pl.DeviceIdType.MESH
F32 = jnp.float32
BF16 = jnp.bfloat16


def iota(shape, axis):
    return lax.broadcasted_iota(jnp.int32, shape, axis)


def unit_phase(turns):
    frac = turns - jnp.round(turns)
    half = frac * math.pi
    sq = half * half
    sin_h = sum_poly(sq, [(-1.0) ** n / math.factorial(2 * n + 1) for n in range(7)]) * half
    cos_h = sum_poly(sq, [(-1.0) ** n / math.factorial(2 * n) for n in range(8)])
    return 1.0 - 2.0 * sin_h * sin_h, 2.0 * sin_h * cos_h


def sum_poly(x, coefs):
    total = jnp.full_like(x, coefs[-1])
    for coef in coefs[-2::-1]:
        total = total * x + coef
    return total


def cmul(a, b):
    return a[0] * b[0] - a[1] * b[1], a[0] * b[1] + a[1] * b[0]


def kernel(
    n_span, n_freq, cap, rows_per, tile_ref, offs_ref, chan_ref, count_ref, coord_ref, vis_ref,
    taper_ref, out_ref, tile_v, offs_v, chan_v, count_v, coord_v, vis_v, taper_v, in_sem, ea, eb,
    ab_scr, g_scr, y_scr, z_scr, rhs_scr, src_v, src_s, send, got, acc_scr,
    rs_send, rs_got, src_sem, a_send, a_recv, r_send, r_recv, g_send, g_recv,
):
    me_s, me_f = lax.axis_index("span"), lax.axis_index("freq")
    barrier = pltpu.get_barrier_semaphore()
    for o in range(1, n_span):
        pl.semaphore_signal(
            barrier, inc=1, device_id=(lax.rem(me_s + o, n_span), me_f), device_id_type=MESH
        )
    for o in range(1, n_freq):
        pl.semaphore_signal(
            barrier, inc=1, device_id=(me_s, lax.rem(me_f + o, n_freq)), device_id_type=MESH
        )

    hbm = [tile_ref, offs_ref, chan_ref, count_ref, coord_ref, vis_ref, taper_ref]
    vmem = [tile_v, offs_v, chan_v, count_v, coord_v, vis_v, taper_v]
    fetch = [
        pltpu.make_async_copy(a, b, in_sem.at[n]) for n, (a, b) in enumerate(zip(hbm, vmem))
    ]
    for copy in fetch:
        copy.start()
    for copy in fetch[:4]:
        copy.wait()
    tile_ref, offs_ref, chan_ref, count_ref, coord_ref, vis_ref, taper_ref = vmem
    kk = coord_ref.shape[2]
    lanes = cap * 32
    data_rows = cap * 16
    slots = n_span * cap

    tile_l, chan_l = tile_ref[...].astype(F32), chan_ref[...].astype(F32)
    row_l, col_l = offs_ref[0:1, :].astype(F32), offs_ref[1:2, :].astype(F32)
    count_l = count_ref[...].astype(F32)
    kind = iota((16, SUB), 0) & 3
    meta = jnp.where(
        kind == 0, jnp.broadcast_to(row_l, (16, SUB)),
        jnp.where(kind == 1, 1.0, jnp.broadcast_to(chan_l, (16, SUB))),
    )
    eye = iota((SUB, SUB), 0) == iota((SUB, SUB), 1)

    def to_rows(row):
        return jnp.sum(
            jnp.where(eye, jnp.broadcast_to(row, (SUB, SUB)), 0.0), axis=1, keepdims=True
        )

    dest_l = tile_l
    dest_s = to_rows(dest_l)
    same = jnp.broadcast_to(dest_l, (SUB, SUB)) == dest_s
    lower = iota((SUB, SUB), 1) < iota((SUB, SUB), 0)
    upper = iota((SUB, SUB), 0) < iota((SUB, SUB), 1)
    rank_s = jnp.sum(jnp.where(same & lower, 1.0, 0.0), axis=1, keepdims=True)
    rank_l = jnp.sum(jnp.where(same & upper, 1.0, 0.0), axis=0, keepdims=True)
    slot_s = (dest_s * cap + rank_s).astype(jnp.int32)
    slot_l = (dest_l * cap + rank_l).astype(jnp.int32)
    hot = jnp.broadcast_to(slot_s, (SUB, 128)) == iota((SUB, 128), 1)
    src = jnp.sum(jnp.where(hot, iota((SUB, 128), 0).astype(F32), 0.0), axis=0, keepdims=True)
    turn_s = to_rows(col_l)
    turn_s = turn_s - 32.0 * jnp.floor(turn_s * (1.0 / 32.0))
    turn = jnp.sum(
        jnp.where(iota((SUB, 128), 0) == iota((SUB, 128), 1), turn_s, 0.0), axis=0, keepdims=True
    )
    src_v[...] = jnp.where(
        iota((8, 128), 0) == 0, jnp.broadcast_to(src, (8, 128)), jnp.broadcast_to(turn, (8, 128))
    ).astype(jnp.int32)
    src_copy = pltpu.make_async_copy(src_v, src_s, src_sem)
    src_copy.start()
    col_s = to_rows(col_l)
    count_s = to_rows(count_l)
    hot_t = jnp.broadcast_to(slot_l, (slots, SUB)) == iota((slots, SUB), 0)
    col_splat = jnp.dot(
        jnp.where(hot_t, 1.0, 0.0).astype(BF16),
        jnp.broadcast_to(col_s, (SUB, 128)).astype(BF16),
        preferred_element_type=F32,
    )
    hot_x = jnp.broadcast_to(slot_s, (SUB, slots * 32)) == iota((SUB, slots * 32), 1) >> 5
    spread_meta = jnp.dot(
        meta.astype(BF16), jnp.where(hot_x, 1.0, 0.0).astype(BF16), preferred_element_type=F32
    )
    eight = iota((8, 128), 0)
    for d in range(n_span):
        cols = col_splat[d * cap:(d + 1) * cap]
        if cap < 8:
            cols = jnp.concatenate([cols, jnp.zeros((8 - cap, 128), F32)], 0)
        info = spread_meta[0:8, d * lanes:d * lanes + 128]
        if lanes > 128:
            info = jnp.where(eight < 4, info, spread_meta[0:8, d * lanes + 128:d * lanes + 256])
        send[d, data_rows:, :] = jnp.concatenate([cols, info], 0).astype(BF16)

    def powers(turns):
        e1 = unit_phase(turns)
        e2 = cmul(e1, e1)
        e3 = cmul(e2, e1)
        e4 = cmul(e2, e2)
        e8 = cmul(e4, e4)
        e16 = cmul(e8, e8)
        return e1, e2, e3, e4, e8, e16

    for copy in fetch[4:]:
        copy.wait()
    piece_lane = iota((8, 128), 1).astype(F32)
    for g in range(SUB // 8):
        rows = slice(8 * g, 8 * g + 8)
        left_over = jnp.broadcast_to(count_s[rows], (8, 128)) - piece_lane
        for kt in range(kk // 128):
            cols = slice(128 * kt, 128 * kt + 128)
            for n, val in enumerate(powers(coord_ref[rows, 0, cols] * (-1.0 / 32.0))):
                ea[rows, 8 * n + kt, :] = val[0]
                ea[rows, 8 * n + 4 + kt, :] = val[1]
            e1, e2, e3, e4, e8, e16 = powers(coord_ref[rows, 1, cols] * (-1.0 / 32.0))
            live = jnp.where(left_over > 128.0 * kt, 1.0 / math.sqrt(kk), 0.0)
            vis = vis_ref[rows, :, cols].astype(F32)
            w0 = (vis[:, 0, :] * live, vis[:, 1, :] * live)
            for n, val in enumerate([w0, cmul(w0, e1), cmul(w0, e2), cmul(w0, e3), e4, e8, e16]):
                eb[rows, 8 * n + kt, :] = val[0]
                eb[rows, 8 * n + 4 + kt, :] = val[1]

    sub8 = iota((8, 128), 0)
    bit0, bit1, bit2 = (sub8 & 1) == 1, (sub8 & 2) == 2, sub8 >= 4
    taper = taper_ref[...]
    taper = jnp.concatenate([taper, taper], 1)
    taper = jnp.concatenate([taper, taper], 0)
    taper = jnp.concatenate([taper, taper], 1)
    low_half64 = iota((64, 128), 1) < 64

    def expand(rows4, e4, e8, e16):
        low = [
            jnp.where(
                bit1, jnp.where(bit0, rows4[3][c], rows4[2][c]),
                jnp.where(bit0, rows4[1][c], rows4[0][c]),
            )
            for c in range(2)
        ]
        base = cmul(low, (jnp.where(bit2, e4[0], 1.0), jnp.where(bit2, e4[1], 0.0)))
        rr, ii = base[0] * e8[0], base[1] * e8[1]
        ri, ir = base[0] * e8[1], base[1] * e8[0]
        first = (base[0] * e16[0] + base[1] * e16[1], base[1] * e16[0] - base[0] * e16[1])
        blocks = [first, (rr + ii, ir - ri), base, (rr - ii, ri + ir)]
        return [
            jnp.concatenate([blocks[2 * half][c], blocks[2 * half + 1][c]], 0).astype(BF16)
            for c in range(2) for half in range(2)
        ]

    group = 8

    def sub_group(i, carry):
        for u in range(group):
            s = i * group + u
            for kt in range(kk // 128):
                cols = slice(128 * kt, 128 * kt + 128)

                def row(ref, n):
                    return tuple(
                        jnp.broadcast_to(ref[s, at:at + 1, :], (8, 128))
                        for at in (8 * n + kt, 8 * n + 4 + kt)
                    )

                one = (jnp.ones((8, 128), F32), jnp.zeros((8, 128), F32))
                a_rows = expand(
                    [one] + [row(ea, n) for n in range(3)], *[row(ea, n) for n in range(3, 6)]
                )
                b_rows = expand(
                    [row(eb, n) for n in range(4)], *[row(eb, n) for n in range(4, 7)]
                )
                for n in range(4):
                    ab_scr[u, 0, 16 * n:16 * n + 16, cols] = a_rows[n]
                    ab_scr[u, 1, 16 * n:16 * n + 16, cols] = b_rows[n]
            grid = lax.dot_general(
                ab_scr[u, 0], ab_scr[u, 1], (((1,), (1,)), ((), ())), preferred_element_type=F32
            )
            wide = jnp.concatenate([grid, grid], 1) * taper
            high = wide.astype(BF16)
            rest = (wide - high.astype(F32)).astype(BF16)
            rows = pl.ds(pl.multiple_of(s * 64, 64), 64)
            g_scr[rows, 0:128] = high
            g_scr[rows, 128:256] = rest
        return carry

    lax.fori_loop(0, SUB // group, sub_group, 0)

    def turns_of(rows, cols):
        prod = ((rows & 31) - 16) * ((cols & 31) - 16)
        return prod.astype(F32) * (-1.0 / 32.0)

    def quarter(n):
        return n.astype(F32) * 0.25

    rows, cols = iota((64, 128), 0), iota((64, 128), 1)
    right = unit_phase(
        turns_of(rows, cols) + quarter((cols >> 6) + (rows >> 5) - ((cols >> 5) & 1))
    )[0]
    right_h = right.astype(BF16)
    right_l = (right - right_h.astype(F32)).astype(BF16)
    right = jnp.concatenate([right_h, right_l, right_h, jnp.zeros((64, 128), BF16)], 0)
    rows, cols = iota((64, 64), 0), iota((64, 64), 1)
    left = unit_phase(turns_of(rows, cols) + quarter((cols >> 5) - (rows >> 5)))[0]
    left = (left * (1.0 / 32.0)).astype(BF16)
    rows, cols = iota((128, 512), 0), iota((128, 512), 1)
    repeat = jnp.where(
        ((rows >> 5) == (cols >> 7)) & ((rows & 31) == (cols & 31)), 1.0, 0.0
    ).astype(BF16)

    y_scr[...] = jnp.dot(g_scr[...], right, preferred_element_type=F32).astype(BF16)
    lane32 = iota((32, 128), 1) & 31
    src_copy.wait()

    def second(s, carry):
        part = jnp.dot(
            left, y_scr[pl.ds(pl.multiple_of(s * 64, 64), 64), :], preferred_element_type=F32
        )
        sub = part[:32] + pltpu.roll(part[32:], 64, 1)
        turn = jnp.clip(src_s[1, s], 0, 31)
        z_scr[s] = jnp.where(
            lane32 >= turn, pltpu.roll(sub, turn, 1), pltpu.roll(sub, turn + 96, 1)
        )
        return carry

    lax.fori_loop(0, SUB, second, 0, unroll=32)

    low_half = iota((32, 128), 1) < 64

    def fill(d):
        for j in range(cap // 2):
            at = d * cap + 2 * j
            left_z = z_scr[jnp.clip(src_s[0, at], 0, SUB - 1)]
            right_z = pltpu.roll(z_scr[jnp.clip(src_s[0, at + 1], 0, SUB - 1)], 64, 1)
            send[d, 32 * j:32 * j + 32, :] = jnp.where(low_half, left_z, right_z).astype(BF16)

    pl.semaphore_wait(barrier, n_span + n_freq - 2)
    moves = []
    for o in range(1, n_span):
        to = lax.rem(me_s + o, n_span)
        fill(to)
        move = pltpu.make_async_remote_copy(
            src_ref=send.at[to], dst_ref=got.at[o - 1], send_sem=a_send.at[o - 1],
            recv_sem=a_recv.at[o - 1], device_id=(to, me_f), device_id_type=MESH,
        )
        move.start()
        moves.append(move)
    fill(me_s)

    channels = CH_DEV * n_freq
    lane = iota((1, 128), 1)
    lane_a = (lane & 31).astype(F32)
    cell_row = iota((TILE, 128), 0).astype(F32)

    def widen(block, n):
        wide = jnp.dot(block[0:data_rows, :], repeat, preferred_element_type=F32)
        info = block[data_rows:, :].astype(F32)
        for i in range(cap):
            j, h = i // 2, i % 2
            off = piece_lane - jnp.broadcast_to(info[i:i + 1, :], (8, 128))
            inside = jnp.where((off >= 0.0) & (off < 32.0), 1.0, 0.0)
            inside = jnp.concatenate([inside] * 4, 0) > 0.5
            part = wide[32 * j:32 * j + 32, 256 * h:256 * h + 256]
            rhs_scr[n, 32 * i:32 * i + 32, 0:128] = jnp.where(
                inside, part[:, :128], 0.0
            ).astype(BF16)
            rhs_scr[n, 32 * i:32 * i + 32, 128:256] = jnp.where(
                inside, part[:, 128:], 0.0
            ).astype(BF16)

    exact = channels & (channels - 1) == 0 and channels <= 256

    def weigh(block, n, term):
        info = block[data_rows:, :].astype(F32)
        high, low = [], []
        for j in range(lanes // 128):
            at = 8 + 4 * j
            hit = cell_row == info[at:at + 1, :] + lane_a
            val = info[at + 1:at + 2, :]
            if term == 1:
                chan = info[at + 2:at + 3, :] + (me_f * CH_DEV).astype(F32)
                val = val * ((2.0 * chan + 1.0 - channels) / channels)
            cut = val.astype(BF16).astype(F32)
            high.append(jnp.where(hit, jnp.broadcast_to(cut, (TILE, 128)), 0.0).astype(BF16))
            low.append(jnp.where(hit, jnp.broadcast_to(val - cut, (TILE, 128)), 0.0).astype(BF16))
        res = jnp.dot(jnp.concatenate(high, 1), rhs_scr[n], preferred_element_type=F32)
        if term == 1 and not exact:
            res = res + jnp.dot(jnp.concatenate(low, 1), rhs_scr[n], preferred_element_type=F32)
        return res

    blocks = [send.at[me_s]] + [got.at[o - 1] for o in range(1, n_span)]
    acc = None
    starts = [0, 1, n_span // 2, n_span]
    for first, last in zip(starts[:-1], starts[1:]):
        for n in range(first, last):
            if n:
                moves[n - 1].wait_recv()
        for n in range(first, last):
            widen(blocks[n], n)
        for n in range(first, last):
            res = weigh(blocks[n], n, 0)
            acc = res if acc is None else acc + res

    def peer_rows(place):
        return pl.ds(pl.multiple_of(place * rows_per, rows_per), rows_per)

    half = 2 * TILE
    pad = n_freq * rows_per - half

    def scatter(acc, term):
        if pad:
            acc_scr[term, half:, :] = jnp.zeros((pad, 128), F32)
            rs_send[term, half:, :] = jnp.zeros((pad, 128), BF16)
        for c in range(2):
            part = acc[:, c * 128:(c + 1) * 128]
            acc_scr[term, c * TILE:(c + 1) * TILE, :] = part
            rs_send[term, c * TILE:(c + 1) * TILE, :] = part.astype(BF16)
        started = []
        for o in range(1, n_freq):
            to = lax.rem(me_f + o, n_freq)
            move = pltpu.make_async_remote_copy(
                src_ref=rs_send.at[term, peer_rows(to)], dst_ref=rs_got.at[term, o - 1],
                send_sem=r_send.at[term, o - 1], recv_sem=r_recv.at[term, o - 1],
                device_id=(me_s, to), device_id_type=MESH,
            )
            move.start()
            started.append(move)
        return started

    sums = [scatter(acc, 0)]
    acc = None
    for n, block in enumerate(blocks):
        res = weigh(block, n, 1)
        acc = res if acc is None else acc + res
    sums.append(scatter(acc, 1))

    scale = TILE / (32.0 * math.sqrt(n_freq * SUB))
    gathers = []
    for term in range(NT):
        total = acc_scr[term, peer_rows(me_f), :]
        for o in range(1, n_freq):
            sums[term][o - 1].wait_recv()
            total = total + rs_got[term, o - 1].astype(F32)
        mine = out_ref.at[term, peer_rows(me_f)]
        mine[...] = (total * scale).astype(BF16)
        started = []
        for o in range(1, n_freq):
            to = lax.rem(me_f + o, n_freq)
            move = pltpu.make_async_remote_copy(
                src_ref=mine, dst_ref=mine,
                send_sem=g_send.at[term, o - 1], recv_sem=g_recv.at[term, o - 1],
                device_id=(me_s, to), device_id_type=MESH,
            )
            move.start()
            started.append(move)
        gathers.append(started)
    for term in range(NT):
        for o in range(1, n_freq):
            gathers[term][o - 1].wait_recv()
    for move in moves + sums[0] + sums[1] + gathers[0] + gathers[1]:
        move.wait_send()


def body(visibilities, coords, vis_counts, cover_tile, offsets, channel, taper):
    n_span = lax.axis_size("span")
    n_freq = lax.axis_size("freq")
    sub = visibilities.shape[1]
    kk = visibilities.shape[-1]
    cap = max(4, 2 * sub // n_span)
    rows_per = -(-2 * TILE // (16 * n_freq)) * 16
    dma = pltpu.SemaphoreType.DMA
    block = cap * 16 + 16
    out = pl.pallas_call(
        functools.partial(kernel, n_span, n_freq, cap, rows_per),
        out_shape=jax.ShapeDtypeStruct((NT, n_freq * rows_per, 128), BF16),
        in_specs=[pl.BlockSpec(memory_space=pltpu.HBM)] * 7,
        out_specs=pl.BlockSpec(memory_space=pltpu.VMEM),
        scratch_shapes=[
            pltpu.VMEM((1, sub), jnp.int32),
            pltpu.VMEM((2, sub), jnp.int32),
            pltpu.VMEM((1, sub), jnp.int32),
            pltpu.VMEM((1, sub), jnp.int32),
            pltpu.VMEM((sub, 2, kk), F32),
            pltpu.VMEM((sub, 2, kk), BF16),
            pltpu.VMEM((32, 32), F32),
            dma((7,)),
            pltpu.VMEM((sub, 48, 128), F32),
            pltpu.VMEM((sub, 56, 128), F32),
            pltpu.VMEM((8, 2, 64, kk), BF16),
            pltpu.VMEM((sub * 64, 256), BF16),
            pltpu.VMEM((sub * 64, 128), BF16),
            pltpu.VMEM((sub, 32, 128), F32),
            pltpu.VMEM((n_span, cap * 32, 256), BF16),
            pltpu.VMEM((8, 128), jnp.int32),
            pltpu.SMEM((8, 128), jnp.int32),
            pltpu.VMEM((n_span, block, 128), BF16),
            pltpu.VMEM((n_span - 1, block, 128), BF16),
            pltpu.VMEM((NT, n_freq * rows_per, 128), F32),
            pltpu.VMEM((NT, n_freq * rows_per, 128), BF16),
            pltpu.VMEM((NT, n_freq - 1, rows_per, 128), BF16),
            dma(()),
            dma((n_span - 1,)), dma((n_span - 1,)),
            dma((NT, n_freq - 1)), dma((NT, n_freq - 1)),
            dma((NT, n_freq - 1)), dma((NT, n_freq - 1)),
        ],
        compiler_params=pltpu.CompilerParams(
            collective_id=0, has_side_effects=True, vmem_limit_bytes=60 * 1024 * 1024
        ),
    )(
        cover_tile[:, :, 0], offsets[0].T, channel, vis_counts, coords[0], visibilities[0], taper,
    )
    return out[:, :2 * TILE].astype(F32).reshape(NT, 1, 2, TILE, TILE)


def solution(mesh):
    return jax.shard_map(
        body,
        mesh=mesh,
        in_specs=(
            P("freq", "span", None, None),
            P("freq", "span", None, None),
            P("freq", "span"),
            P("freq", "span", None),
            P("freq", "span", None),
            P("freq", "span"),
            P(),
        ),
        out_specs=P(None, "span", None, None, None),
        check_vma=False,
    )
```

```python
import functools
import math

import jax
import jax.numpy as jnp
from jax import lax
from jax.experimental import pallas as pl
from jax.experimental.pallas import tpu as pltpu
from jax.sharding import PartitionSpec as P

TILE = 128
NT = 2
CH_DEV = 16
SUB = 32
MESH = pl.DeviceIdType.MESH
F32 = jnp.float32
BF16 = jnp.bfloat16


def iota(shape, axis):
    return lax.broadcasted_iota(jnp.int32, shape, axis)


def unit_phase(turns):
    frac = turns - jnp.round(turns)
    half = frac * math.pi
    sq = half * half
    sin_h = sum_poly(sq, [(-1.0) ** n / math.factorial(2 * n + 1) for n in range(7)]) * half
    cos_h = sum_poly(sq, [(-1.0) ** n / math.factorial(2 * n) for n in range(8)])
    return 1.0 - 2.0 * sin_h * sin_h, 2.0 * sin_h * cos_h


def sum_poly(x, coefs):
    total = jnp.full_like(x, coefs[-1])
    for coef in coefs[-2::-1]:
        total = total * x + coef
    return total


def cmul(a, b):
    return a[0] * b[0] - a[1] * b[1], a[0] * b[1] + a[1] * b[0]


def kernel(
    n_span, n_freq, cap, rows_per, tile_ref, offs_ref, chan_ref, count_ref, coord_ref, vis_ref,
    taper_ref, out_ref, ea, eb, g_scr, y_scr, z_scr, rhs_scr, src_v, src_s, send, got, acc_scr,
    rs_send, rs_got, src_sem, a_send, a_recv, r_send, r_recv, g_send, g_recv,
):
    me_s, me_f = lax.axis_index("span"), lax.axis_index("freq")
    barrier = pltpu.get_barrier_semaphore()
    for o in range(1, n_span):
        pl.semaphore_signal(
            barrier, inc=1, device_id=(lax.rem(me_s + o, n_span), me_f), device_id_type=MESH
        )
    for o in range(1, n_freq):
        pl.semaphore_signal(
            barrier, inc=1, device_id=(me_s, lax.rem(me_f + o, n_freq)), device_id_type=MESH
        )

    kk = coord_ref.shape[2]
    lanes = cap * 32
    data_rows = cap * 16
    slots = n_span * cap

    tile_l, chan_l = tile_ref[...].astype(F32), chan_ref[...].astype(F32)
    row_l, col_l = offs_ref[0:1, :].astype(F32), offs_ref[1:2, :].astype(F32)
    count_l = count_ref[...].astype(F32)
    kind = iota((16, SUB), 0) & 3
    meta = jnp.where(
        kind == 0, jnp.broadcast_to(row_l, (16, SUB)),
        jnp.where(kind == 1, 1.0, jnp.broadcast_to(chan_l, (16, SUB))),
    )
    eye = iota((SUB, SUB), 0) == iota((SUB, SUB), 1)

    def to_rows(row):
        return jnp.sum(
            jnp.where(eye, jnp.broadcast_to(row, (SUB, SUB)), 0.0), axis=1, keepdims=True
        )

    dest_l = tile_l
    dest_s = to_rows(dest_l)
    same = jnp.broadcast_to(dest_l, (SUB, SUB)) == dest_s
    lower = iota((SUB, SUB), 1) < iota((SUB, SUB), 0)
    upper = iota((SUB, SUB), 0) < iota((SUB, SUB), 1)
    rank_s = jnp.sum(jnp.where(same & lower, 1.0, 0.0), axis=1, keepdims=True)
    rank_l = jnp.sum(jnp.where(same & upper, 1.0, 0.0), axis=0, keepdims=True)
    slot_s = (dest_s * cap + rank_s).astype(jnp.int32)
    slot_l = (dest_l * cap + rank_l).astype(jnp.int32)
    hot = jnp.broadcast_to(slot_s, (SUB, 128)) == iota((SUB, 128), 1)
    src = jnp.sum(jnp.where(hot, iota((SUB, 128), 0).astype(F32), 0.0), axis=0, keepdims=True)
    turn_s = to_rows(col_l)
    turn_s = turn_s - 32.0 * jnp.floor(turn_s * (1.0 / 32.0))
    turn = jnp.sum(
        jnp.where(iota((SUB, 128), 0) == iota((SUB, 128), 1), turn_s, 0.0), axis=0, keepdims=True
    )
    src_v[...] = jnp.where(
        iota((8, 128), 0) == 0, jnp.broadcast_to(src, (8, 128)), jnp.broadcast_to(turn, (8, 128))
    ).astype(jnp.int32)
    src_copy = pltpu.make_async_copy(src_v, src_s, src_sem)
    src_copy.start()
    col_s = to_rows(col_l)
    count_s = to_rows(count_l)
    hot_t = jnp.broadcast_to(slot_l, (slots, SUB)) == iota((slots, SUB), 0)
    col_splat = jnp.dot(
        jnp.where(hot_t, 1.0, 0.0).astype(BF16),
        jnp.broadcast_to(col_s, (SUB, 128)).astype(BF16),
        preferred_element_type=F32,
    )
    hot_x = jnp.broadcast_to(slot_s, (SUB, slots * 32)) == iota((SUB, slots * 32), 1) >> 5
    spread_meta = jnp.dot(
        meta.astype(BF16), jnp.where(hot_x, 1.0, 0.0).astype(BF16), preferred_element_type=F32
    )
    eight = iota((8, 128), 0)
    for d in range(n_span):
        cols = col_splat[d * cap:(d + 1) * cap]
        if cap < 8:
            cols = jnp.concatenate([cols, jnp.zeros((8 - cap, 128), F32)], 0)
        info = spread_meta[0:8, d * lanes:d * lanes + 128]
        if lanes > 128:
            info = jnp.where(eight < 4, info, spread_meta[0:8, d * lanes + 128:d * lanes + 256])
        send[d, data_rows:, :] = jnp.concatenate([cols, info], 0).astype(BF16)

    def powers(turns):
        e1 = unit_phase(turns)
        e2 = cmul(e1, e1)
        e3 = cmul(e2, e1)
        e4 = cmul(e2, e2)
        e8 = cmul(e4, e4)
        e16 = cmul(e8, e8)
        return e1, e2, e3, e4, e8, e16

    def phases(i, carry):
        rows = pl.ds(pl.multiple_of(i * 8, 8), 8)
        for n, val in enumerate(powers(coord_ref[rows, 0, :] * (-1.0 / 32.0))):
            ea[2 * n, rows, :] = val[0]
            ea[2 * n + 1, rows, :] = val[1]
        return carry

    lax.fori_loop(0, SUB // 8, phases, 0)
    e1, e2, e3, e4, e8, e16 = powers(coord_ref[:, 1, :] * (-1.0 / 32.0))
    live = jnp.where(
        iota((SUB, kk), 1).astype(F32) < jnp.broadcast_to(count_s, (SUB, kk)),
        1.0 / math.sqrt(kk), 0.0,
    )
    vis = vis_ref[...].astype(F32)
    w0 = (vis[:, 0, :] * live, vis[:, 1, :] * live)
    for n, val in enumerate([w0, cmul(w0, e1), cmul(w0, e2), cmul(w0, e3), e4, e8, e16]):
        eb[2 * n] = val[0]
        eb[2 * n + 1] = val[1]

    sub8 = iota((8, kk), 0)
    bit0, bit1, bit2 = (sub8 & 1) == 1, (sub8 & 2) == 2, sub8 >= 4
    taper = taper_ref[...]
    taper = jnp.concatenate([taper, taper], 1)
    taper = jnp.concatenate([taper, taper], 0)
    taper = jnp.concatenate([taper, taper], 1)
    low_half64 = iota((64, 128), 1) < 64

    def expand(rows4, e4, e8, e16):
        low = [
            jnp.where(
                bit1, jnp.where(bit0, rows4[3][c], rows4[2][c]),
                jnp.where(bit0, rows4[1][c], rows4[0][c]),
            )
            for c in range(2)
        ]
        base = cmul(low, (jnp.where(bit2, e4[0], 1.0), jnp.where(bit2, e4[1], 0.0)))
        rr, ii = base[0] * e8[0], base[1] * e8[1]
        ri, ir = base[0] * e8[1], base[1] * e8[0]
        first = (base[0] * e16[0] + base[1] * e16[1], base[1] * e16[0] - base[0] * e16[1])
        blocks = [first, (rr + ii, ir - ri), base, (rr - ii, ri + ir)]
        return jnp.concatenate(
            [b[0] for b in blocks] + [b[1] for b in blocks], 0
        ).astype(BF16)

    def one_sub(s, carry):
        def row(ref, n):
            return tuple(
                jnp.broadcast_to(ref[2 * n + c, pl.ds(s, 1), :], (8, kk)) for c in range(2)
            )

        one = (jnp.ones((8, kk), F32), jnp.zeros((8, kk), F32))
        a_cat = expand([one] + [row(ea, n) for n in range(3)], *[row(ea, n) for n in range(3, 6)])
        b_cat = expand([row(eb, n) for n in range(4)], *[row(eb, n) for n in range(4, 7)])
        grid = lax.dot_general(
            a_cat, b_cat, (((1,), (1,)), ((), ())), preferred_element_type=F32
        )
        wide = jnp.concatenate([grid, grid], 1) * taper
        high = wide.astype(BF16)
        rest = (wide - high.astype(F32)).astype(BF16)
        rows = pl.ds(pl.multiple_of(s * 64, 64), 64)
        g_scr[rows, 0:128] = high
        g_scr[rows, 128:256] = rest
        return carry

    lax.fori_loop(0, SUB, one_sub, 0, unroll=4)

    def turns_of(rows, cols):
        prod = ((rows & 31) - 16) * ((cols & 31) - 16)
        return prod.astype(F32) * (-1.0 / 32.0)

    def quarter(n):
        return n.astype(F32) * 0.25

    rows, cols = iota((64, 128), 0), iota((64, 128), 1)
    right = unit_phase(
        turns_of(rows, cols) + quarter((cols >> 6) + (rows >> 5) - ((cols >> 5) & 1))
    )[0]
    right_h = right.astype(BF16)
    right_l = (right - right_h.astype(F32)).astype(BF16)
    right = jnp.concatenate([right_h, right_l, right_h, jnp.zeros((64, 128), BF16)], 0)
    rows, cols = iota((64, 64), 0), iota((64, 64), 1)
    left = unit_phase(turns_of(rows, cols) + quarter((cols >> 5) - (rows >> 5)))[0]
    left = (left * (1.0 / 32.0)).astype(BF16)
    rows, cols = iota((128, 512), 0), iota((128, 512), 1)
    repeat = jnp.where(
        ((rows >> 5) == (cols >> 7)) & ((rows & 31) == (cols & 31)), 1.0, 0.0
    ).astype(BF16)

    y_scr[...] = jnp.dot(g_scr[...], right, preferred_element_type=F32).astype(BF16)
    lane32 = iota((32, 128), 1) & 31
    src_copy.wait()

    def second(s, carry):
        part = jnp.dot(
            left, y_scr[pl.ds(pl.multiple_of(s * 64, 64), 64), :], preferred_element_type=F32
        )
        sub = part[:32] + pltpu.roll(part[32:], 64, 1)
        turn = jnp.clip(src_s[1, s], 0, 31)
        z_scr[s] = jnp.where(
            lane32 >= turn, pltpu.roll(sub, turn, 1), pltpu.roll(sub, turn + 96, 1)
        )
        return carry

    lax.fori_loop(0, SUB, second, 0, unroll=32)

    low_half = iota((32, 128), 1) < 64

    def fill(d):
        for j in range(cap // 2):
            at = d * cap + 2 * j
            left_z = z_scr[jnp.clip(src_s[0, at], 0, SUB - 1)]
            right_z = pltpu.roll(z_scr[jnp.clip(src_s[0, at + 1], 0, SUB - 1)], 64, 1)
            send[d, 32 * j:32 * j + 32, :] = jnp.where(low_half, left_z, right_z).astype(BF16)

    pl.semaphore_wait(barrier, n_span + n_freq - 2)
    moves = []
    for o in range(1, n_span):
        to = lax.rem(me_s + o, n_span)
        fill(to)
        move = pltpu.make_async_remote_copy(
            src_ref=send.at[to], dst_ref=got.at[o - 1], send_sem=a_send.at[o - 1],
            recv_sem=a_recv.at[o - 1], device_id=(to, me_f), device_id_type=MESH,
        )
        move.start()
        moves.append(move)
    fill(me_s)

    channels = CH_DEV * n_freq
    lane = iota((1, 128), 1)
    lane_a = (lane & 31).astype(F32)
    cell_row = iota((TILE, 128), 0).astype(F32)
    cell_col = iota((8, 128), 1).astype(F32)

    def widen(block, n):
        wide = jnp.dot(block[0:data_rows, :], repeat, preferred_element_type=F32)
        info = block[data_rows:, :].astype(F32)
        for i in range(cap):
            j, h = i // 2, i % 2
            off = cell_col - jnp.broadcast_to(info[i:i + 1, :], (8, 128))
            inside = jnp.where((off >= 0.0) & (off < 32.0), 1.0, 0.0)
            inside = jnp.concatenate([inside] * 4, 0) > 0.5
            part = wide[32 * j:32 * j + 32, 256 * h:256 * h + 256]
            rhs_scr[n, 32 * i:32 * i + 32, 0:128] = jnp.where(
                inside, part[:, :128], 0.0
            ).astype(BF16)
            rhs_scr[n, 32 * i:32 * i + 32, 128:256] = jnp.where(
                inside, part[:, 128:], 0.0
            ).astype(BF16)

    exact = channels & (channels - 1) == 0 and channels <= 256

    def weigh(block, n, term):
        info = block[data_rows:, :].astype(F32)
        high, low = [], []
        for j in range(lanes // 128):
            at = 8 + 4 * j
            hit = cell_row == info[at:at + 1, :] + lane_a
            val = info[at + 1:at + 2, :]
            if term == 1:
                chan = info[at + 2:at + 3, :] + (me_f * CH_DEV).astype(F32)
                val = val * ((2.0 * chan + 1.0 - channels) / channels)
            cut = val.astype(BF16).astype(F32)
            high.append(jnp.where(hit, jnp.broadcast_to(cut, (TILE, 128)), 0.0).astype(BF16))
            low.append(jnp.where(hit, jnp.broadcast_to(val - cut, (TILE, 128)), 0.0).astype(BF16))
        res = jnp.dot(jnp.concatenate(high, 1), rhs_scr[n], preferred_element_type=F32)
        if term == 1 and not exact:
            res = res + jnp.dot(jnp.concatenate(low, 1), rhs_scr[n], preferred_element_type=F32)
        return res

    blocks = [send.at[me_s]] + [got.at[o - 1] for o in range(1, n_span)]
    acc = None
    for n, block in enumerate(blocks):
        if n:
            moves[n - 1].wait_recv()
        widen(block, n)
        res = weigh(block, n, 0)
        acc = res if acc is None else acc + res

    def peer_rows(place):
        return pl.ds(pl.multiple_of(place * rows_per, rows_per), rows_per)

    half = 2 * TILE
    pad = n_freq * rows_per - half

    def scatter(acc, term):
        if pad:
            acc_scr[term, half:, :] = jnp.zeros((pad, 128), F32)
            rs_send[term, half:, :] = jnp.zeros((pad, 128), BF16)
        for c in range(2):
            part = acc[:, c * 128:(c + 1) * 128]
            acc_scr[term, c * TILE:(c + 1) * TILE, :] = part
            rs_send[term, c * TILE:(c + 1) * TILE, :] = part.astype(BF16)
        started = []
        for o in range(1, n_freq):
            to = lax.rem(me_f + o, n_freq)
            move = pltpu.make_async_remote_copy(
                src_ref=rs_send.at[term, peer_rows(to)], dst_ref=rs_got.at[term, o - 1],
                send_sem=r_send.at[term, o - 1], recv_sem=r_recv.at[term, o - 1],
                device_id=(me_s, to), device_id_type=MESH,
            )
            move.start()
            started.append(move)
        return started

    sums = [scatter(acc, 0)]
    acc = None
    for n, block in enumerate(blocks):
        res = weigh(block, n, 1)
        acc = res if acc is None else acc + res
    sums.append(scatter(acc, 1))

    scale = TILE / (32.0 * math.sqrt(n_freq * SUB))
    gathers = []
    for term in range(NT):
        total = acc_scr[term, peer_rows(me_f), :]
        for o in range(1, n_freq):
            sums[term][o - 1].wait_recv()
            total = total + rs_got[term, o - 1].astype(F32)
        mine = out_ref.at[term, peer_rows(me_f)]
        mine[...] = (total * scale).astype(BF16)
        started = []
        for o in range(1, n_freq):
            to = lax.rem(me_f + o, n_freq)
            move = pltpu.make_async_remote_copy(
                src_ref=mine, dst_ref=mine,
                send_sem=g_send.at[term, o - 1], recv_sem=g_recv.at[term, o - 1],
                device_id=(me_s, to), device_id_type=MESH,
            )
            move.start()
            started.append(move)
        gathers.append(started)
    for term in range(NT):
        for o in range(1, n_freq):
            gathers[term][o - 1].wait_recv()
    for move in moves + sums[0] + sums[1] + gathers[0] + gathers[1]:
        move.wait_send()


def body(visibilities, coords, vis_counts, cover_tile, offsets, channel, taper):
    n_span = lax.axis_size("span")
    n_freq = lax.axis_size("freq")
    sub = visibilities.shape[1]
    kk = visibilities.shape[-1]
    cap = max(4, 2 * sub // n_span)
    rows_per = -(-2 * TILE // (16 * n_freq)) * 16
    dma = pltpu.SemaphoreType.DMA
    block = cap * 16 + 16
    out = pl.pallas_call(
        functools.partial(kernel, n_span, n_freq, cap, rows_per),
        out_shape=jax.ShapeDtypeStruct((NT, n_freq * rows_per, 128), BF16),
        in_specs=[pl.BlockSpec(memory_space=pltpu.VMEM)] * 7,
        out_specs=pl.BlockSpec(memory_space=pltpu.VMEM),
        scratch_shapes=[
            pltpu.VMEM((12, sub, kk), F32),
            pltpu.VMEM((14, sub, kk), F32),
            pltpu.VMEM((sub * 64, 256), BF16),
            pltpu.VMEM((sub * 64, 128), BF16),
            pltpu.VMEM((sub, 32, 128), F32),
            pltpu.VMEM((n_span, cap * 32, 256), BF16),
            pltpu.VMEM((8, 128), jnp.int32),
            pltpu.SMEM((8, 128), jnp.int32),
            pltpu.VMEM((n_span, block, 128), BF16),
            pltpu.VMEM((n_span - 1, block, 128), BF16),
            pltpu.VMEM((NT, n_freq * rows_per, 128), F32),
            pltpu.VMEM((NT, n_freq * rows_per, 128), BF16),
            pltpu.VMEM((NT, n_freq - 1, rows_per, 128), BF16),
            dma(()),
            dma((n_span - 1,)), dma((n_span - 1,)),
            dma((NT, n_freq - 1)), dma((NT, n_freq - 1)),
            dma((NT, n_freq - 1)), dma((NT, n_freq - 1)),
        ],
        compiler_params=pltpu.CompilerParams(
            collective_id=0, has_side_effects=True, vmem_limit_bytes=32 * 1024 * 1024
        ),
    )(
        cover_tile[:, :, 0], offsets[0].T, channel, vis_counts, coords[0], visibilities[0], taper,
    )
    return out[:, :2 * TILE].astype(F32).reshape(NT, 1, 2, TILE, TILE)


def solution(mesh):
    return jax.shard_map(
        body,
        mesh=mesh,
        in_specs=(
            P("freq", "span", None, None),
            P("freq", "span", None, None),
            P("freq", "span"),
            P("freq", "span", None),
            P("freq", "span", None),
            P("freq", "span"),
            P(),
        ),
        out_specs=P(None, "span", None, None, None),
        check_vma=False,
    )
```
